128 devices in a mesh: ep: 128 (over y, z, x, core).
Axes of the slice: x: 4, y: 4, z: 4, core: 2. Of those that a mesh axis runs over, the one named last changes fastest.
Arguments:
- queries: bfloat16 [1, 2048, 64, 576], P(None, 'ep'), may hold values from -320 to 320
- latent_cache: bfloat16 [2048, 128, 576], P('ep'), may hold values from -4 to 4
- new_latent: bfloat16 [1, 2048, 576], P(None, 'ep'), may hold values from -4 to 4
- lengths: int32 [2048], P('ep'), may hold values from 16 to 128
- hidden: bfloat16 [1, 2048, 3584], P(None, 'ep'), may hold values from -400 to 400
- norm_gain: float32 [3584], replicated, may hold values from 0.1 to 1.9
- routes: int32 [1, 2048, 8], P(None, 'ep'), may hold values from 0 to 127, all different within a row; in each aligned block of 16 rows (0 to 15, 16 to 31, ..., all dimensions but the last counted through in order) at most 3 rows name the same one
- route_weight: float32 [1, 2048, 8], P(None, 'ep'), may hold values from 0.1 to 1
- gate_weight: bfloat16 [128, 3584, 1024], P('ep'), may hold values from -0.09375 to 0.09375
- up_weight: bfloat16 [128, 3584, 1024], P('ep'), may hold values from -0.09375 to 0.09375
- down_weight: bfloat16 [128, 1024, 3584], P('ep'), may hold values from -0.1875 to 0.1875
Outputs:
- attended: bfloat16 [1, 2048, 64, 512], P(None, 'ep')
- expert_mix: bfloat16 [1, 2048, 3584], P(None, 'ep')
The draws below stay inside these ranges and needn't reach their ends.
Inputs may be any that keep to these rules, and one draw needn't show every extreme that they name: `routes`: each token names 8 different experts; among the rows of one device in one step no expert is named more than 3 times.
All inputs are finite; a program needn't handle non-finite values.
Results may differ from the reference program's by a relative error of at most 0.0071.
Values may be sent and summed in bfloat16 or wider, within the bound.
A program may use at most 128 MiB of HBM per device.

```python
import math
import jax
import jax.numpy as jnp
import numpy as np
from jax import lax

D = 3584
FF = 1024
HEADS = 64
LAT = 512
ROPE = 64
KDIM = 576
TOPK = 8
STEPS = 1
CTX = 128
ROWS_DEV = 16
MOST = 3
ROWS = 2048
EXPERTS = 128
N_EP = 128


def key_table(key):
    table_key = jax.random.fold_in(key, 11)
    normal_part = jnp.clip(jax.random.normal(table_key, (ROWS, CTX, LAT + ROPE), jnp.float32), -4.0, 4.0)
    table = normal_part
    copied = table[:, 9, LAT:]
    return table.at[:, 9, LAT:].set(copied)


def draw_latent_cache(key, part):
    table = key_table(key)
    return table.astype(jnp.bfloat16)


def draw_queries(key, part):
    own_key = jax.random.fold_in(key, 13)
    base = jnp.clip(jax.random.normal(own_key, (STEPS, ROWS, HEADS, LAT + ROPE), jnp.float32), -4.0, 4.0)
    return base.astype(jnp.bfloat16)


def draw_lengths(key, part):
    key = jax.random.fold_in(key, 3)
    key_long, key_short = jax.random.split(key)
    row_ids = jnp.arange(ROWS)
    heavy = row_ids // ROWS_DEV < N_EP // 2
    long_draw = jax.random.randint(key_long, (ROWS,), CTX // 2, CTX + 1)
    short_draw = jax.random.randint(key_short, (ROWS,), 16, CTX // 8 + 1)
    picked = jnp.where(heavy, long_draw, short_draw)
    picked = picked.at[0].set(CTX).at[ROWS - 1].set(16)
    return picked.astype(jnp.int32)


def draw_hidden(key, part):
    key = jax.random.fold_in(key, 5)
    key_col, key_row, key_base = jax.random.split(key, 3)
    column_scale = jnp.exp(jax.random.uniform(key_col, (D,), jnp.float32, 0.0, 2.302585))
    row_scale = jnp.exp(jax.random.uniform(key_row, (STEPS, ROWS, 1), jnp.float32, 0.0, 2.302585))
    base = jnp.clip(jax.random.normal(key_base, (STEPS, ROWS, D), jnp.float32), -4.0, 4.0)
    values = base * column_scale * row_scale
    return values.astype(jnp.bfloat16)


def levels(key, dims, cuts, least, largest):
    gain, own = 1.0, jax.random.fold_in(key, 6)
    for dim, parts in cuts:
        heights = jnp.exp(jax.random.uniform(jax.random.fold_in(own, dim), (parts,), jnp.float32, least / len(cuts), largest / len(cuts)))
        gain = gain * jnp.repeat(heights, dims[dim] // parts).reshape([-1 if axis == dim else 1 for axis in range(len(dims))])
    return gain


def deal_out(stream_key, own, number, rows, count, top, reach, slope):
    sequence = jax.random.permutation(stream_key, count)
    crowded, ordinary = load_shares(count, rows * top, reach, slope, True), load_shares(count, rows * top, reach, slope, False)
    places = jnp.arange(count)

    def named(sizes, rotation):
        used = int((sizes > 0).sum())
        fixed = max(1, used // 4)
        passed = fixed + (places - fixed + rotation * (used - fixed)) % max(1, count - fixed)
        return jnp.zeros((count,), jnp.int32).at[sequence[jnp.where(places < fixed, places, passed)]].set(jnp.asarray(sizes, jnp.int32))

    sizes = jnp.where(number % 4 == 0, named(crowded, number // 4), named(ordinary, number - number // 4 - 1))
    mixed = jax.random.permutation(jax.random.fold_in(own, 3), count)
    donor, taker = mixed[0:count // 2 * 2:2], mixed[1:count // 2 * 2:2]
    room = jnp.minimum(sizes[donor] - 1, reach - sizes[taker]) // 2
    room = jnp.where((donor == sequence[0]) | (taker == sequence[0]) | (sizes[taker] == 0), 0, jnp.maximum(room, 0))
    passed = jax.random.randint(jax.random.fold_in(own, 4), (count // 2,), 0, 1 << 20) % (room + 1)
    sizes = sizes.at[donor].add(-passed).at[taker].add(passed)
    members = jnp.searchsorted(jnp.cumsum(sizes), jnp.arange(rows * top), side="right").astype(jnp.int32)
    listing = members.reshape(top, rows).T
    listing = listing[jax.random.permutation(jax.random.fold_in(own, 1), rows)]
    rotation = jax.random.randint(jax.random.fold_in(own, 2), (rows, 1), 0, top)
    return jnp.take_along_axis(listing, (jnp.arange(top)[None, :] + rotation) % top, axis=1)


def load_shares(count, total, most, lean, full):
    weights = [(1 << 20) // math.isqrt(rank ** lean) + 1 for rank in range(1, count + 1)]
    largest = most if full else min(most, max(-(-total // count), total * weights[0] // sum(weights)))
    least = 1 if total - largest >= count - 1 else 0
    given, spare = [largest] + [least] * (count - 1), total - largest - least * (count - 1)
    while spare > 0:
        free = [i for i in range(1, count) if given[i] < largest] or [i for i in range(1, count) if given[i] < most]
        pool, remaining = sum([weights[i] for i in free]), spare
        for i in free:
            addition = min(most - given[i], max(1, remaining * weights[i] // pool), spare)
            given[i] = given[i] + addition
            spare = spare - addition
    return np.array(given)


def normal_values(key, dims, scale, reach, shards=(), kind=jnp.bfloat16):
    drawn = scale * jax.random.normal(key, dims, jnp.float32)
    if shards:
        drawn = drawn * levels(key, dims, shards, -0.22, 0.18)
    return jnp.clip(drawn, -reach, reach).astype(kind)


def setup_inputs(seed: int = 0) -> dict:
    arg_keys = jax.random.split(jax.random.key(seed), 12)
    queries = draw_queries(jax.random.fold_in(arg_keys[11], 71), 0)
    latent_cache = draw_latent_cache(jax.random.fold_in(arg_keys[11], 71), 0)
    new_latent = normal_values(arg_keys[2], (STEPS, ROWS, KDIM), 1.0, 4.0, ((1, 128),))
    lengths = draw_lengths(jax.random.fold_in(arg_keys[11], 71), 0)
    hidden = draw_hidden(jax.random.fold_in(arg_keys[11], 71), 0)
    norm_gain = jnp.clip(1.0 + 0.18 * jax.random.normal(arg_keys[5], (D,), jnp.float32), 0.1, 1.9)
    routes_keys = jax.random.split(jax.random.fold_in(arg_keys[6], 1), STEPS * ROWS // ROWS_DEV)
    routes_turns = jax.random.permutation(jax.random.fold_in(arg_keys[6], 3), STEPS * ROWS // ROWS_DEV)
    routes = jax.vmap(lambda own, number: deal_out(jax.random.fold_in(arg_keys[6], 2), own, number, ROWS_DEV, N_EP, TOPK, MOST, 2))(routes_keys, routes_turns).reshape((STEPS, ROWS, TOPK))
    route_weight = jnp.clip(0.1 + 0.9 * jax.random.uniform(arg_keys[7], (STEPS, ROWS, TOPK), jnp.float32) ** levels(arg_keys[7], (STEPS, ROWS, TOPK), ((1, 128),), -0.2, 0.2), 0.1, 1.0)
    gate_weight = normal_values(arg_keys[8], (EXPERTS, D, FF), D ** -0.5, 0.09375, ((0, 128),))
    up_weight = normal_values(arg_keys[9], (EXPERTS, D, FF), D ** -0.5, 0.09375, ((0, 128),))
    down_weight = normal_values(arg_keys[10], (EXPERTS, FF, D), FF ** -0.5, 0.1875, ((0, 128),))
    return dict(queries=queries, latent_cache=latent_cache, new_latent=new_latent, lengths=lengths, hidden=hidden, norm_gain=norm_gain, routes=routes, route_weight=route_weight, gate_weight=gate_weight, up_weight=up_weight, down_weight=down_weight)


soft_scale = 192.0 ** (-0.5)
neg_large = -1e+30
tile_rows = 64

def rounded(values):
    return lax.optimization_barrier(values.astype(jnp.bfloat16)).astype(jnp.float32)

def attend_row(packed):
    query_row, cache_row, fresh_row, length = packed
    query_f = query_row.astype(jnp.float32)
    cache_f = cache_row.astype(jnp.float32)
    fresh_f = fresh_row.astype(jnp.float32)
    cache_scores = jnp.einsum('shk,ck->shc', query_f, cache_f) * soft_scale
    positions = jnp.arange(CTX, dtype=jnp.int32)
    cache_scores = jnp.where(positions[None, None, :] < length, cache_scores, neg_large)
    fresh_scores = jnp.einsum('shk,tk->sht', query_f, fresh_f) * soft_scale
    step_ids = jnp.arange(STEPS, dtype=jnp.int32)
    fresh_scores = jnp.where(step_ids[None, None, :] <= step_ids[:, None, None], fresh_scores, neg_large)
    row_max = jnp.maximum(lax.optimization_barrier(jnp.max(cache_scores, axis=2)), lax.optimization_barrier(jnp.max(fresh_scores, axis=2)))
    cache_weights = jnp.exp(cache_scores - row_max[:, :, None])
    fresh_weights = jnp.exp(fresh_scores - row_max[:, :, None])
    total_weight = lax.optimization_barrier(jnp.sum(cache_weights, axis=2)) + lax.optimization_barrier(jnp.sum(fresh_weights, axis=2))
    summed = jnp.einsum('shc,cl->shl', rounded(cache_weights), cache_f[:, :LAT])
    summed = summed + jnp.einsum('sht,tl->shl', rounded(fresh_weights), fresh_f[:, :LAT])
    return (summed / total_weight[:, :, None]).astype(jnp.bfloat16)

def reference(queries, latent_cache, new_latent, lengths, hidden, norm_gain, routes, route_weight, gate_weight, up_weight, down_weight):
    attended = lax.map(attend_row, (jnp.swapaxes(queries, 0, 1), latent_cache, jnp.swapaxes(new_latent, 0, 1), lengths))
    attended = jnp.swapaxes(attended, 0, 1)
    hidden_f = hidden.astype(jnp.float32)
    mean_square = lax.optimization_barrier(jnp.mean(hidden_f * hidden_f, axis=-1, keepdims=True))
    normed = (hidden_f * lax.rsqrt(mean_square + 1e-06) * norm_gain).astype(jnp.bfloat16)
    tokens = normed.reshape(STEPS * ROWS, D)
    expert_ids = routes.reshape(-1).astype(jnp.int32)
    pair_weights = route_weight.reshape(-1)
    pair_total = expert_ids.shape[0]
    pair_order = jnp.argsort(expert_ids, stable=True).astype(jnp.int32)
    counts = lax.optimization_barrier(jnp.sum((expert_ids[:, None] == jnp.arange(EXPERTS, dtype=jnp.int32)[None, :]).astype(jnp.int32), axis=0))
    starts = jnp.cumsum(counts) - counts
    tile_counts = (counts + tile_rows - 1) // tile_rows
    tile_ends = jnp.cumsum(tile_counts)
    tile_starts = tile_ends - tile_counts
    tile_total = (pair_total + tile_rows - 1) // tile_rows + EXPERTS

    def one_tile(mix_sum, tile_index):
        expert = jnp.minimum(jnp.sum((tile_ends <= tile_index).astype(jnp.int32)), EXPERTS - 1).astype(jnp.int32)
        within = (tile_index - tile_starts[expert]) * tile_rows + jnp.arange(tile_rows, dtype=jnp.int32)
        active = (within >= 0) & (within < counts[expert]) & (tile_index < tile_ends[EXPERTS - 1])
        pair_ids = pair_order[jnp.clip(starts[expert] + within, 0, pair_total - 1)]
        token_rows = pair_ids // TOPK
        inputs = tokens[token_rows]
        gate_part = jnp.dot(inputs, gate_weight[expert], preferred_element_type=jnp.float32)
        up_part = jnp.dot(inputs, up_weight[expert], preferred_element_type=jnp.float32)
        hidden_units = (jax.nn.silu(gate_part) * up_part).astype(jnp.bfloat16)
        output = jnp.dot(hidden_units, down_weight[expert], preferred_element_type=jnp.float32).astype(jnp.bfloat16)
        scaled = jnp.where(active, pair_weights[pair_ids], 0.0)[:, None] * output.astype(jnp.float32)
        return (mix_sum.at[token_rows].add(scaled), None)
    start_sum = jnp.zeros((STEPS * ROWS, D), jnp.float32)
    mix_sum, unused = lax.scan(one_tile, start_sum, jnp.arange(tile_total, dtype=jnp.int32))
    expert_mix = mix_sum.astype(jnp.bfloat16).reshape(STEPS, ROWS, D)
    return (attended, expert_mix)
```

```python
import functools

import jax
import jax.numpy as jnp
import numpy as np
from jax import lax
from jax.experimental import pallas as pl
from jax.experimental.pallas import tpu as pltpu
from jax.sharding import PartitionSpec as P

MESH = pl.DeviceIdType.MESH
F32, BF16 = jnp.float32, jnp.bfloat16

D, FF, HEADS, LAT, KDIM, TOPK, CTX, ROWS = 3584, 1024, 64, 512, 576, 8, 128, 16
MOST = 3
SIDE = 4
SLOTS = MOST * SIDE * SIDE
LINE = 2 * SIDE
ALL = SLOTS * LINE
META = 128
soft_scale = 192.0 ** (-0.5)
neg_large = -1e30

PARTS = ((0, 1280, (0, 1, 2)), (1280, 1152, (1, 2, 0)), (2432, 1152, (2, 0, 1)))
STRIDES = (32, 8, 2)


def slot_orders():
    def row(k1, k2, k3, kc, j):
        return (k3 * 2 + kc) * SLOTS + j * SIDE * SIDE + k2 * SIDE + k1

    turns = np.zeros((2, ALL, ALL), np.float32)
    for ky in range(SIDE):
        for kz in range(SIDE):
            for kx in range(SIDE):
                for kc in range(2):
                    for j in range(MOST):
                        k = (ky, kz, kx)
                        rows = [row(k[o[0]], k[o[1]], k[o[2]], kc, j) for _, _, o in PARTS]
                        turns[0, rows[0], rows[1]] = 1
                        turns[1, rows[0], rows[2]] = 1
    return turns


def dot(a, b):
    return jnp.dot(a, b, preferred_element_type=F32)


def dot_t(a, b):
    return lax.dot_general(a, b, (((1,), (1,)), ((), ())), preferred_element_type=F32)


def kernel(
    lengths, fresh, hidden, gain, routes, route_weight, queries, cache, turns, gate_w, up_w, down_w,
    attended, mix,
    q_buf, c_buf, att_buf, turn_buf, wg, wu, wd,
    g1a, g1b, g1c, g2a, g2b, g2c, sa, sb, sc, ra, rb, rc, oa, ob, oc, ca, cb, cc,
    p2a, p2b, p2c, f2a, f2b, f2c, p1a, p1b, p1c, f1a, f1b, f1c,
    pick, mix_hi, mix_lo, tokens, inner,
    local_sem, send_sem, recv_sem,
):
    g1, g2, sel, got, outs, back = (g1a, g1b, g1c), (g2a, g2b, g2c), (sa, sb, sc), (ra, rb, rc), (oa, ob, oc), (ca, cb, cc)
    p2, f2, p1, f1 = (p2a, p2b, p2c), (f2a, f2b, f2c), (p1a, p1b, p1c), (f1a, f1b, f1c)

    me = lax.axis_index("ep")
    place = (me // 32, (me // 8) % 4, (me // 2) % 4)
    core = me % 2

    def device(dim, step, core_step=0):
        moved = (place[dim] + step) % SIDE
        other = (core + core_step) % 2
        return me + (moved - place[dim]) * STRIDES[dim] + (other - core)

    loads = [
        pltpu.make_async_copy(queries.at[0], q_buf, local_sem.at[0]),
        pltpu.make_async_copy(cache, c_buf, local_sem.at[1]),
        pltpu.make_async_copy(gate_w.at[0], wg, local_sem.at[2]),
        pltpu.make_async_copy(up_w.at[0], wu, local_sem.at[3]),
        pltpu.make_async_copy(turns, turn_buf, local_sem.at[4]),
        pltpu.make_async_copy(down_w.at[0], wd, local_sem.at[5]),
    ]
    for load in loads:
        load.start()

    barrier = pltpu.get_barrier_semaphore()
    partners = [device(dim, step, c) for dim in range(3) for step in range(1, SIDE) for c in range(2)]
    partners.append(device(0, 0, 1))
    for partner in partners:
        pl.semaphore_signal(barrier, inc=1, device_id=(partner,), device_id_type=MESH)

    hidden_f = hidden[0].astype(F32)
    mean_square = jnp.mean(hidden_f * hidden_f, axis=-1, keepdims=True)
    normed = (hidden_f * lax.rsqrt(mean_square + 1e-06) * gain[...]).astype(BF16)
    lanes = lax.broadcasted_iota(jnp.int32, (ROWS, META), 1)
    route_now = routes[0]
    weight_now = route_weight[0]
    named = [lanes == route_now[:, k : k + 1] for k in range(TOPK)]
    taken = sum(hit.astype(F32) for hit in named)
    earlier = lax.broadcasted_iota(jnp.int32, (ROWS, ROWS), 0) > lax.broadcasted_iota(jnp.int32, (ROWS, ROWS), 1)
    before = dot(earlier.astype(BF16), taken.astype(BF16))
    meta = jnp.zeros((ROWS, META), F32)
    for k in range(TOPK):
        rank = jnp.sum(jnp.where(named[k], before, 0.0), axis=1, keepdims=True)
        weight = weight_now[:, k : k + 1]
        high = weight.astype(BF16).astype(F32)
        meta = jnp.where(lanes == k, route_now[:, k : k + 1].astype(F32), meta)
        meta = jnp.where(lanes == TOPK + k, rank, meta)
        meta = jnp.where(lanes == 2 * TOPK + k, high, meta)
        meta = jnp.where(lanes == 3 * TOPK + k, weight - high, meta)
    meta = meta.astype(BF16)
    for p, (first, width, _) in enumerate(PARTS):
        g1[p][0:ROWS, 0:width] = normed[:, first : first + width]
        g1[p][0:ROWS, width : width + META] = meta

    pl.semaphore_wait(barrier, len(partners))

    def remote(src, dst, p, number, target):
        return pltpu.make_async_remote_copy(
            src_ref=src, dst_ref=dst, send_sem=send_sem.at[p, number], recv_sem=recv_sem.at[p, number],
            device_id=(target,), device_id_type=MESH,
        )

    def block(ref, number, rows):
        return ref.at[pl.ds(number * rows, rows)]

    first_hops = []
    for p, (_, _, order) in enumerate(PARTS):
        hops = [
            remote(block(g1[p], 0, ROWS), block(g1[p], k, ROWS), p, k - 1, device(order[0], k)) for k in (2, 1, 3)
        ]
        for hop in hops:
            hop.start()
        first_hops.append(hops)

    loads[0].wait()
    loads[1].wait()

    def attend(row, unused):
        q = q_buf[row]
        keys = c_buf[row]
        new = fresh[0]
        scores = dot_t(q, keys) * soft_scale
        scores = jnp.where(lax.broadcasted_iota(jnp.int32, (HEADS, CTX), 1) < lengths[row], scores, neg_large)
        new_scores = dot_t(q, new) * soft_scale
        new_scores = jnp.where(lax.broadcasted_iota(jnp.int32, (HEADS, ROWS), 1) == row, new_scores, neg_large)
        most = jnp.maximum(jnp.max(scores, axis=1, keepdims=True), jnp.max(new_scores, axis=1, keepdims=True))
        weight = jnp.exp(scores - most)
        new_weight = jnp.exp(new_scores - most)
        total = jnp.sum(weight, axis=1, keepdims=True) + jnp.sum(new_weight, axis=1, keepdims=True)
        summed = dot(weight.astype(BF16), keys[:, :LAT]) + dot(new_weight.astype(BF16), new[:, :LAT])
        att_buf[row] = (summed / total).astype(BF16)
        return unused

    lax.fori_loop(0, 4, attend, 0)

    second_hops = []
    for p, (_, _, order) in enumerate(PARTS):
        for hop in first_hops[p]:
            hop.wait_recv()
        g2[p][0:64, :] = g1[p][...]
        hops = [
            remote(block(g2[p], 0, 64), block(g2[p], k, 64), p, 2 + k, device(order[1], k)) for k in (2, 1, 3)
        ]
        for hop in hops:
            hop.start()
        second_hops.append(hops)

    lax.fori_loop(4, 12, attend, 0)

    def targets(p, shape, dim):
        order = PARTS[p][2]
        index = lax.broadcasted_iota(jnp.int32, shape, dim)
        goal = jnp.zeros(shape, jnp.int32)
        for number in range(LINE):
            expert = device(order[2], number // 2, number % 2)
            inside = index - number * SLOTS
            rank = (inside >= 16).astype(jnp.int32) + (inside >= 32).astype(jnp.int32)
            code = (inside - rank * 16) * 512 + expert * 4 + rank
            goal = jnp.where((inside >= 0) & (inside < SLOTS), code, goal)
        return goal.astype(F32)

    third_hops = []
    for p, (_, width, order) in enumerate(PARTS):
        for hop in second_hops[p]:
            hop.wait_recv()
        meta_all = g2[p][:, width : width + META].astype(F32)
        meta_t = jnp.transpose(meta_all)
        home = (lax.broadcasted_iota(jnp.int32, (TOPK, 256), 1) // 16) * 512
        codes = meta_t[0:TOPK] * 4.0 + meta_t[TOPK : 2 * TOPK] + home.astype(F32)
        goal = targets(p, (ALL, 1), 0)
        hit = jnp.zeros((ALL, 256), F32)
        for k in range(TOPK):
            hit = jnp.where(codes[k : k + 1] == goal, 1.0, hit)
        pick[...] = hit.astype(BF16)
        picked = dot(pick[...], g2[p][:, 0:width]).astype(BF16)
        got[p][0:SLOTS, :] = picked[0:SLOTS]
        sel[p][...] = picked[SLOTS:]
        hops = []
        for number in (4, 5, 2, 3, 6, 7, 1):
            hop = remote(
                block(sel[p], number - 1, SLOTS), block(got[p], number, SLOTS), p, 5 + number,
                device(order[2], number // 2, number % 2),
            )
            hop.start()
            hops.append(hop)
        third_hops.append(hops)

    for p, (_, width, order) in enumerate(PARTS):
        meta_all = g2[p][:, width : width + META].astype(F32)
        home = (lax.broadcasted_iota(jnp.int32, (256, 1), 0) // 16) * 512
        goal = targets(p, (1, ALL), 1)
        share = jnp.zeros((256, ALL), F32)
        for k in range(TOPK):
            code = meta_all[:, k : k + 1] * 4.0 + meta_all[:, TOPK + k : TOPK + k + 1] + home.astype(F32)
            weight = meta_all[:, 2 * TOPK + k : 2 * TOPK + k + 1] + meta_all[:, 3 * TOPK + k : 3 * TOPK + k + 1]
            share = jnp.where(code == goal, weight, share)
        high = share.astype(BF16)
        mix_hi[p] = high
        mix_lo[p] = (share - high.astype(F32)).astype(BF16)

    lax.fori_loop(12, ROWS, attend, 0)
    store = pltpu.make_async_copy(att_buf, attended.at[0], local_sem.at[6])
    store.start()

    loads[4].wait()
    for p, (first, width, _) in enumerate(PARTS):
        for hop in third_hops[p]:
            hop.wait_recv()
        rows = got[p][...]
        if p:
            rows = dot(turn_buf[p - 1], rows).astype(BF16)
        tokens[:, first : first + width] = rows
    loads[2].wait()
    loads[3].wait()

    def units(tile, unused):
        columns = pl.ds(pl.multiple_of(tile * 256, 256), 256)
        gate = dot(tokens[...], wg[:, columns])
        up = dot(tokens[...], wu[:, columns])
        inner[:, columns] = (gate / (1.0 + jnp.exp(-gate)) * up).astype(BF16)
        return unused

    lax.fori_loop(0, FF // 256, units, 0)
    loads[5].wait()

    back_hops = []
    for p, (first, width, order) in enumerate(PARTS):
        rows = inner[...]
        if p:
            rows = dot(turn_buf[2 - p], rows).astype(BF16)
        result = dot(rows, wd[:, first : first + width]).astype(BF16)
        back[p][0:SLOTS, :] = result[0:SLOTS]
        outs[p][...] = result[SLOTS:]
        hops = []
        for number in (4, 5, 2, 3, 6, 7, 1):
            hop = remote(
                block(outs[p], number - 1, SLOTS), block(back[p], number, SLOTS), p, 12 + number,
                device(order[2], -(number // 2), number % 2),
            )
            hop.start()
            hops.append(hop)
        back_hops.append(hops)

    late_hops = []
    for p, (_, width, order) in enumerate(PARTS):
        for hop in back_hops[p]:
            hop.wait_recv()
        summed = (dot(mix_hi[p], back[p][...]) + dot(mix_lo[p], back[p][...])).astype(BF16)
        f2[p][0:64, :] = summed[0:64]
        p2[p][...] = summed[64:]
        hops = [
            remote(block(p2[p], k - 1, 64), block(f2[p], k, 64), p, 19 + k, device(order[1], -k)) for k in (2, 1, 3)
        ]
        for hop in hops:
            hop.start()
        late_hops.append(hops)

    last_hops = []
    for p, (_, width, order) in enumerate(PARTS):
        for hop in late_hops[p]:
            hop.wait_recv()
        summed = sum(f2[p][64 * k : 64 * k + 64, :].astype(F32) for k in range(SIDE)).astype(BF16)
        f1[p][0:ROWS, :] = summed[0:ROWS]
        p1[p][...] = summed[ROWS:]
        hops = [
            remote(block(p1[p], k - 1, ROWS), block(f1[p], k, ROWS), p, 22 + k, device(order[0], -k)) for k in (2, 1, 3)
        ]
        for hop in hops:
            hop.start()
        last_hops.append(hops)

    for p, (first, width, _) in enumerate(PARTS):
        for hop in last_hops[p]:
            hop.wait_recv()
        summed = sum(f1[p][ROWS * k : ROWS * k + ROWS, :].astype(F32) for k in range(SIDE))
        mix[0, :, first : first + width] = summed.astype(BF16)

    for hops in first_hops + second_hops + third_hops + back_hops + late_hops + last_hops:
        for hop in hops:
            hop.wait_send()
    store.wait()


def on_device(
    queries, latent_cache, new_latent, lengths, hidden, norm_gain, routes, route_weight, gate_weight, up_weight,
    down_weight,
):
    def per_part(rows, extra=0):
        return [pltpu.VMEM((rows, width + extra), BF16) for _, width, _ in PARTS]

    vmem = pl.BlockSpec(memory_space=pltpu.VMEM)
    smem = pl.BlockSpec(memory_space=pltpu.SMEM)
    hbm = pl.BlockSpec(memory_space=pl.ANY)
    turns = jnp.asarray(slot_orders(), BF16)
    return pl.pallas_call(
        kernel,
        out_shape=(
            jax.ShapeDtypeStruct((1, ROWS, HEADS, LAT), BF16),
            jax.ShapeDtypeStruct((1, ROWS, D), BF16),
        ),
        in_specs=[smem, vmem, vmem, vmem, vmem, vmem] + [hbm] * 6,
        out_specs=(hbm, vmem),
        scratch_shapes=[
            pltpu.VMEM((ROWS, HEADS, KDIM), BF16),
            pltpu.VMEM((ROWS, CTX, KDIM), BF16),
            pltpu.VMEM((ROWS, HEADS, LAT), BF16),
            pltpu.VMEM((2, ALL, ALL), BF16),
            pltpu.VMEM((D, FF), BF16),
            pltpu.VMEM((D, FF), BF16),
            pltpu.VMEM((FF, D), BF16),
            *per_part(64, META),
            *per_part(256, META),
            *per_part(ALL - SLOTS),
            *per_part(ALL),
            *per_part(ALL - SLOTS),
            *per_part(ALL),
            *per_part(192),
            *per_part(256),
            *per_part(48),
            *per_part(64),
            pltpu.VMEM((ALL, 256), BF16),
            pltpu.VMEM((3, 256, ALL), BF16),
            pltpu.VMEM((3, 256, ALL), BF16),
            pltpu.VMEM((ALL, D), BF16),
            pltpu.VMEM((ALL, FF), BF16),
            pltpu.SemaphoreType.DMA((7,)),
            pltpu.SemaphoreType.DMA((3, 26)),
            pltpu.SemaphoreType.DMA((3, 26)),
        ],
        compiler_params=pltpu.CompilerParams(
            collective_id=0, has_side_effects=True, vmem_limit_bytes=61 * 2**20
        ),
    )(
        lengths, new_latent, hidden, norm_gain.reshape(1, D), routes, route_weight, queries, latent_cache, turns,
        gate_weight, up_weight, down_weight,
    )


def solution(mesh):
    placed = (
        P(None, "ep", None, None),
        P("ep", None, None),
        P(None, "ep", None),
        P("ep"),
        P(None, "ep", None),
        P(),
        P(None, "ep", None),
        P(None, "ep", None),
        P("ep", None, None),
        P("ep", None, None),
        P("ep", None, None),
    )
    return jax.shard_map(
        on_device,
        mesh=mesh,
        in_specs=placed,
        out_specs=(P(None, "ep", None, None), P(None, "ep", None)),
        check_vma=False,
    )
```

```python
import functools

import jax
import jax.numpy as jnp
import numpy as np
from jax import lax
from jax.experimental import pallas as pl
from jax.experimental.pallas import tpu as pltpu
from jax.sharding import PartitionSpec as P

MESH = pl.DeviceIdType.MESH
F32, BF16 = jnp.float32, jnp.bfloat16

D, FF, HEADS, LAT, KDIM, TOPK, CTX, ROWS = 3584, 1024, 64, 512, 576, 8, 128, 16
MOST = 3
SIDE = 4
SLOTS = MOST * SIDE * SIDE
LINE = 2 * SIDE
ALL = SLOTS * LINE
META = 128
soft_scale = 192.0 ** (-0.5)
neg_large = -1e30

ORDERS = ((0, 1, 2), (1, 2, 0), (2, 0, 1))
PARTS = (
    (0, 640, 0), (640, 640, 1), (1280, 640, 2),
    (1920, 640, 0), (2560, 512, 1), (3072, 512, 2),
)
STRIDES = (32, 8, 2)
HALF = ALL // 2


def slot_orders():
    def row(k1, k2, k3, j):
        return k3 * SLOTS + j * SIDE * SIDE + k2 * SIDE + k1

    turns = np.zeros((2, HALF, HALF), np.float32)
    for ky in range(SIDE):
        for kz in range(SIDE):
            for kx in range(SIDE):
                for j in range(MOST):
                    k = (ky, kz, kx)
                    rows = [row(k[o[0]], k[o[1]], k[o[2]], j) for o in ORDERS]
                    turns[0, rows[0], rows[1]] = 1
                    turns[1, rows[0], rows[2]] = 1
    return turns


def dot(a, b):
    return jnp.dot(a, b, preferred_element_type=F32)


def dot_t(a, b):
    return lax.dot_general(a, b, (((1,), (1,)), ((), ())), preferred_element_type=F32)


def kernel(
    lengths, fresh, hidden, gain, routes, route_weight, queries, cache, turns, gate_w, up_w, down_w,
    attended, mix,
    q_buf, c_buf, att_buf, turn_buf, wg, wu, wd, *rest,
):
    count = len(PARTS)
    g1, g2, sel, got, outs, back, p2, f2, p1, f1, sums = (rest[i * count : (i + 1) * count] for i in range(11))
    pick, mix_hi, mix_lo, tokens, inner, local_sem, send_sem, recv_sem = rest[11 * count :]

    me = lax.axis_index("ep")
    place = (me // 32, (me // 8) % 4, (me // 2) % 4)
    core = me % 2

    def device(dim, step, core_step=0):
        moved = (place[dim] + step) % SIDE
        other = (core + core_step) % 2
        return me + (moved - place[dim]) * STRIDES[dim] + (other - core)

    loads = [
        pltpu.make_async_copy(queries.at[0], q_buf, local_sem.at[0]),
        pltpu.make_async_copy(cache, c_buf, local_sem.at[1]),
        pltpu.make_async_copy(gate_w.at[0], wg, local_sem.at[2]),
        pltpu.make_async_copy(up_w.at[0], wu, local_sem.at[3]),
        pltpu.make_async_copy(turns, turn_buf, local_sem.at[4]),
        pltpu.make_async_copy(down_w.at[0], wd, local_sem.at[5]),
    ]
    for load in loads:
        load.start()

    barrier = pltpu.get_barrier_semaphore()
    partners = [device(dim, step, c) for dim in range(3) for step in range(1, SIDE) for c in range(2)]
    partners.append(device(0, 0, 1))
    for partner in partners:
        pl.semaphore_signal(barrier, inc=1, device_id=(partner,), device_id_type=MESH)

    hidden_f = hidden[0].astype(F32)
    mean_square = jnp.mean(hidden_f * hidden_f, axis=-1, keepdims=True)
    normed = (hidden_f * lax.rsqrt(mean_square + 1e-06) * gain[...].reshape(1, D)).astype(BF16)
    lanes = lax.broadcasted_iota(jnp.int32, (ROWS, META), 1)
    both = jnp.concatenate([routes[0].astype(F32), route_weight[0]], axis=0)
    both = jnp.transpose(both)
    route_now = both[:, 0:TOPK].astype(jnp.int32)
    weight_now = both[:, TOPK : 2 * TOPK]
    named = [lanes == route_now[:, k : k + 1] for k in range(TOPK)]
    taken = sum(hit.astype(F32) for hit in named)
    earlier = lax.broadcasted_iota(jnp.int32, (ROWS, ROWS), 0) > lax.broadcasted_iota(jnp.int32, (ROWS, ROWS), 1)
    before = dot(earlier.astype(BF16), taken.astype(BF16))
    meta = jnp.zeros((ROWS, META), F32)
    for k in range(TOPK):
        rank = jnp.sum(jnp.where(named[k], before, 0.0), axis=1, keepdims=True)
        weight = weight_now[:, k : k + 1]
        high = weight.astype(BF16).astype(F32)
        meta = jnp.where(lanes == k, route_now[:, k : k + 1].astype(F32), meta)
        meta = jnp.where(lanes == TOPK + k, rank, meta)
        meta = jnp.where(lanes == 2 * TOPK + k, high, meta)
        meta = jnp.where(lanes == 3 * TOPK + k, weight - high, meta)
    meta = meta.astype(BF16)
    for p, (first, width, _) in enumerate(PARTS):
        g1[p][0:ROWS, 0:width] = normed[:, first : first + width]
        if p < 3:
            g1[p][0:ROWS, width : width + META] = meta

    pl.semaphore_wait(barrier, len(partners))

    def remote(src, dst, p, number, target):
        return pltpu.make_async_remote_copy(
            src_ref=src, dst_ref=dst, send_sem=send_sem.at[p, number], recv_sem=recv_sem.at[p, number],
            device_id=(target,), device_id_type=MESH,
        )

    def block(ref, number, rows):
        return ref.at[pl.ds(number * rows, rows)]

    first_hops, second_hops = [], []
    for p, (_, _, which) in enumerate(PARTS):
        order = ORDERS[which]
        first_hops.append([
            remote(block(g1[p], 0, ROWS), block(g1[p], k, ROWS), p, k - 1, device(order[0], k)) for k in (2, 1, 3)
        ])
        for hop in first_hops[p]:
            hop.start()
    for p, (_, _, which) in enumerate(PARTS):
        order = ORDERS[which]
        second_hops.append([
            remote(block(g1[p], 0, ROWS), g2[p].at[pl.ds(64 * k, ROWS)], p, 2 + k, device(order[1], k)) for k in (2, 1, 3)
        ])
        for hop in second_hops[p]:
            hop.start()

    loads[0].wait()
    loads[1].wait()

    def attend(row, unused):
        q = q_buf[row]
        keys = c_buf[row]
        new = fresh[0]
        scores = dot(q, keys) * soft_scale
        scores = jnp.where(lax.broadcasted_iota(jnp.int32, (HEADS, CTX), 1) < lengths[row], scores, neg_large)
        new_scores = dot_t(q, new) * soft_scale
        new_scores = jnp.where(lax.broadcasted_iota(jnp.int32, (HEADS, ROWS), 1) == row, new_scores, neg_large)
        most = jnp.maximum(jnp.max(scores, axis=1, keepdims=True), jnp.max(new_scores, axis=1, keepdims=True))
        weight = jnp.exp(scores - most)
        new_weight = jnp.exp(new_scores - most)
        total = jnp.sum(weight, axis=1, keepdims=True) + jnp.sum(new_weight, axis=1, keepdims=True)
        summed = dot_t(weight.astype(BF16), keys[:LAT]) + dot(new_weight.astype(BF16), new[:, :LAT])
        att_buf[row] = (summed / total).astype(BF16)
        return unused

    lax.fori_loop(0, 4, attend, 0)

    for p, (_, _, which) in enumerate(PARTS):
        order = ORDERS[which]
        for hop in first_hops[p]:
            hop.wait_recv()
        hops = [
            remote(
                g1[p].at[pl.ds(ROWS, 48)], g2[p].at[pl.ds(64 * k + ROWS, 48)], p, 5 + k, device(order[1], k)
            ) for k in (2, 1, 3)
        ]
        for hop in hops:
            hop.start()
        second_hops[p] += hops
        g2[p][0:64, :] = g1[p][...]

    lax.fori_loop(4, 12, attend, 0)

    def targets(which, shape, dim):
        index = lax.broadcasted_iota(jnp.int32, shape, dim)
        goal = jnp.zeros(shape, jnp.int32)
        for number in range(LINE):
            expert = device(ORDERS[which][2], number % SIDE, number // SIDE)
            inside = index - number * SLOTS
            rank = (inside >= 16).astype(jnp.int32) + (inside >= 32).astype(jnp.int32)
            code = (inside - rank * 16) * 512 + expert * 4 + rank
            goal = jnp.where((inside >= 0) & (inside < SLOTS), code, goal)
        return goal.astype(F32)

    third_hops = [[[], []] for _ in PARTS]

    def send_picked(p, half):
        order = ORDERS[PARTS[p][2]]
        width = PARTS[p][1]
        picked = dot(pick[p % 3, half * HALF : half * HALF + HALF, :], g2[p][:, 0:width]).astype(BF16)
        if half == 0:
            got[p][0:SLOTS, :] = picked[0:SLOTS]
            sel[p][0 : HALF - SLOTS, :] = picked[SLOTS:]
        else:
            sel[p][HALF - SLOTS :, :] = picked
        for step in (2, 1, 3) if half == 0 else (2, 1, 3, 0):
            number = half * SIDE + step
            hop = remote(
                block(sel[p], number - 1, SLOTS), block(got[p], number, SLOTS), p, 8 + number,
                device(order[2], step, half),
            )
            hop.start()
            third_hops[p][half].append(hop)

    for p, (_, width, which) in enumerate(PARTS):
        for hop in second_hops[p]:
            hop.wait_recv()
        if p < 3:
            meta_t = jnp.transpose(g2[p][:, width : width + META].astype(F32))
            home = (lax.broadcasted_iota(jnp.int32, (TOPK, 256), 1) // 16) * 512
            codes = meta_t[0:TOPK] * 4.0 + meta_t[TOPK : 2 * TOPK] + home.astype(F32)
            goal = targets(which, (ALL, 1), 0)
            hit = jnp.zeros((ALL, 256), F32)
            for k in range(TOPK):
                hit = jnp.where(codes[k : k + 1] == goal, 1.0, hit)
            pick[p] = hit.astype(BF16)
        send_picked(p, 0)
    for p in range(count):
        send_picked(p, 1)

    for p, (_, width, which) in enumerate(PARTS[:3]):
        meta_all = g2[p][:, width : width + META].astype(F32)
        home = (lax.broadcasted_iota(jnp.int32, (256, 1), 0) // 16) * 512
        goal = targets(which, (1, ALL), 1)
        share = jnp.zeros((256, ALL), F32)
        for k in range(TOPK):
            code = meta_all[:, k : k + 1] * 4.0 + meta_all[:, TOPK + k : TOPK + k + 1] + home.astype(F32)
            weight = meta_all[:, 2 * TOPK + k : 2 * TOPK + k + 1] + meta_all[:, 3 * TOPK + k : 3 * TOPK + k + 1]
            share = jnp.where(code == goal, weight, share)
        high = share.astype(BF16)
        low = (share - high.astype(F32)).astype(BF16)
        for half in range(2):
            mix_hi[p, half] = high[:, half * HALF : half * HALF + HALF]
            mix_lo[p, half] = low[:, half * HALF : half * HALF + HALF]

    lax.fori_loop(12, ROWS, attend, 0)
    store = pltpu.make_async_copy(att_buf, attended.at[0], local_sem.at[6])
    store.start()

    loads[4].wait()
    back_hops = [[[], []] for _ in PARTS]
    for half in range(2):
        rows_now = slice(half * HALF, half * HALF + HALF)
        for p, (first, width, which) in enumerate(PARTS):
            for hop in third_hops[p][half]:
                hop.wait_recv()
            rows = got[p][rows_now, :]
            if which:
                rows = dot(turn_buf[which - 1], rows).astype(BF16)
            tokens[:, first : first + width] = rows
        if half == 0:
            loads[2].wait()
            loads[3].wait()

        def units(tile, unused):
            columns = pl.ds(pl.multiple_of(tile * 256, 256), 256)
            gate = dot(tokens[...], wg[:, columns])
            up = dot(tokens[...], wu[:, columns])
            inner[0, :, columns] = (gate / (1.0 + jnp.exp(-gate)) * up).astype(BF16)
            return unused

        lax.fori_loop(0, FF // 256, units, 0)
        if half == 0:
            loads[5].wait()
        for which in (1, 2):
            inner[which] = dot(turn_buf[2 - which], inner[0]).astype(BF16)
        for p, (first, width, which) in enumerate(PARTS):
            order = ORDERS[which]
            result = dot(inner[which], wd[:, first : first + width]).astype(BF16)
            if half == 0:
                back[p][0:SLOTS, :] = result[0:SLOTS]
                outs[p][0 : HALF - SLOTS, :] = result[SLOTS:]
            else:
                outs[p][HALF - SLOTS :, :] = result
            for step in (2, 1, 3) if half == 0 else (2, 1, 3, 0):
                number = half * SIDE + step
                hop = remote(
                    block(outs[p], number - 1, SLOTS), block(back[p], number, SLOTS), p, 16 + number,
                    device(order[2], -step, half),
                )
                hop.start()
                back_hops[p][half].append(hop)

    def relay_sum(p, half):
        for hop in back_hops[p][half]:
            hop.wait_recv()
        rows = back[p][half * HALF : half * HALF + HALF, :]
        return dot(mix_hi[p % 3, half], rows) + dot(mix_lo[p % 3, half], rows)

    for p in range(count):
        sums[p][...] = relay_sum(p, 0)
    late_hops = []
    for p, (_, width, which) in enumerate(PARTS):
        summed = (sums[p][...] + relay_sum(p, 1)).astype(BF16)
        f2[p][0:64, :] = summed[0:64]
        p2[p][...] = summed[64:]
        hops = [
            remote(block(p2[p], k - 1, 64), block(f2[p], k, 64), p, 23 + k, device(ORDERS[which][1], -k))
            for k in (2, 1, 3)
        ]
        for hop in hops:
            hop.start()
        late_hops.append(hops)

    last_hops = []
    for p, (_, width, which) in enumerate(PARTS):
        for hop in late_hops[p]:
            hop.wait_recv()
        summed = sum(f2[p][64 * k : 64 * k + 64, :].astype(F32) for k in range(SIDE)).astype(BF16)
        f1[p][0:ROWS, :] = summed[0:ROWS]
        p1[p][...] = summed[ROWS:]
        hops = [
            remote(block(p1[p], k - 1, ROWS), block(f1[p], k, ROWS), p, 26 + k, device(ORDERS[which][0], -k))
            for k in (2, 1, 3)
        ]
        for hop in hops:
            hop.start()
        last_hops.append(hops)

    for p, (first, width, _) in enumerate(PARTS):
        for hop in last_hops[p]:
            hop.wait_recv()
        summed = sum(f1[p][ROWS * k : ROWS * k + ROWS, :].astype(F32) for k in range(SIDE))
        mix[0, :, first : first + width] = summed.astype(BF16)

    halves = [hops for both in third_hops + back_hops for hops in both]
    for hops in first_hops + second_hops + halves + late_hops + last_hops:
        for hop in hops:
            hop.wait_send()
    store.wait()


def on_device(
    queries, latent_cache, new_latent, lengths, hidden, norm_gain, routes, route_weight, gate_weight, up_weight,
    down_weight,
):
    def per_part(rows, extra=0, dtype=BF16):
        return [
            pltpu.VMEM((rows, width + (extra if p < 3 else 0)), dtype) for p, (_, width, _) in enumerate(PARTS)
        ]

    vmem = pl.BlockSpec(memory_space=pltpu.VMEM)
    smem = pl.BlockSpec(memory_space=pltpu.SMEM)
    hbm = pl.BlockSpec(memory_space=pl.ANY)
    turns = jnp.asarray(slot_orders(), BF16)
    return pl.pallas_call(
        kernel,
        out_shape=(
            jax.ShapeDtypeStruct((1, ROWS, HEADS, LAT), BF16),
            jax.ShapeDtypeStruct((1, ROWS, D), BF16),
        ),
        in_specs=[smem, vmem, vmem, vmem, vmem, vmem] + [hbm] * 6,
        out_specs=(hbm, vmem),
        scratch_shapes=[
            pltpu.VMEM((ROWS, HEADS, KDIM), BF16),
            pltpu.VMEM((ROWS, KDIM, CTX), BF16),
            pltpu.VMEM((ROWS, HEADS, LAT), BF16),
            pltpu.VMEM((2, HALF, HALF), BF16),
            pltpu.VMEM((D, FF), BF16),
            pltpu.VMEM((D, FF), BF16),
            pltpu.VMEM((FF, D), BF16),
            *per_part(64, META),
            *per_part(256, META),
            *per_part(ALL - SLOTS),
            *per_part(ALL),
            *per_part(ALL - SLOTS),
            *per_part(ALL),
            *per_part(192),
            *per_part(256),
            *per_part(48),
            *per_part(64),
            *per_part(256, dtype=F32),
            pltpu.VMEM((3, ALL, 256), BF16),
            pltpu.VMEM((3, 2, 256, HALF), BF16),
            pltpu.VMEM((3, 2, 256, HALF), BF16),
            pltpu.VMEM((HALF, D), BF16),
            pltpu.VMEM((3, HALF, FF), BF16),
            pltpu.SemaphoreType.DMA((7,)),
            pltpu.SemaphoreType.DMA((6, 30)),
            pltpu.SemaphoreType.DMA((6, 30)),
        ],
        compiler_params=pltpu.CompilerParams(
            collective_id=0, has_side_effects=True, vmem_limit_bytes=61 * 2**20
        ),
    )(
        lengths, new_latent, hidden, norm_gain, jnp.swapaxes(routes, 1, 2), jnp.swapaxes(route_weight, 1, 2), queries,
        jnp.swapaxes(latent_cache, 1, 2), turns, gate_weight, up_weight, down_weight,
    )


def solution(mesh):
    placed = (
        P(None, "ep", None, None),
        P("ep", None, None),
        P(None, "ep", None),
        P("ep"),
        P(None, "ep", None),
        P(),
        P(None, "ep", None),
        P(None, "ep", None),
        P("ep", None, None),
        P("ep", None, None),
        P("ep", None, None),
    )
    return jax.shard_map(
        on_device,
        mesh=mesh,
        in_specs=placed,
        out_specs=(P(None, "ep", None, None), P(None, "ep", None)),
        check_vma=False,
    )
```

```python
import functools

import jax
import jax.numpy as jnp
import numpy as np
from jax import lax
from jax.experimental import pallas as pl
from jax.experimental.pallas import tpu as pltpu
from jax.sharding import PartitionSpec as P

MESH = pl.DeviceIdType.MESH
F32, BF16 = jnp.float32, jnp.bfloat16

D, FF, HEADS, LAT, KDIM, TOPK, CTX, ROWS = 3584, 1024, 64, 512, 576, 8, 128, 16
MOST = 3
SIDE = 4
SLOTS = MOST * SIDE * SIDE
LINE = 2 * SIDE
ALL = SLOTS * LINE
META = 128
soft_scale = 192.0 ** (-0.5)
neg_large = -1e30

ORDERS = ((0, 1, 2), (1, 2, 0), (2, 0, 1))
PARTS = ((0, 1280), (1280, 1152), (2432, 1152))
NEAR = 640
STRIDES = (32, 8, 2)
HALF = ALL // 2


def slot_orders():
    def row(k1, k2, k3, j):
        return k3 * SLOTS + j * SIDE * SIDE + k2 * SIDE + k1

    turns = np.zeros((2, HALF, HALF), np.float32)
    for ky in range(SIDE):
        for kz in range(SIDE):
            for kx in range(SIDE):
                for j in range(MOST):
                    k = (ky, kz, kx)
                    rows = [row(k[o[0]], k[o[1]], k[o[2]], j) for o in ORDERS]
                    turns[0, rows[0], rows[1]] = 1
                    turns[1, rows[0], rows[2]] = 1
    return turns


def dot(a, b):
    return jnp.dot(a, b, preferred_element_type=F32)


def dot_t(a, b):
    return lax.dot_general(a, b, (((1,), (1,)), ((), ())), preferred_element_type=F32)


def kernel(
    lengths, fresh, hidden, gain, routes, route_weight, queries, cache, turns, gate_w, up_w, down_w,
    attended, mix,
    q_buf, c_buf, att_buf, turn_buf, wg, wu, wd, *rest,
):
    count = len(PARTS)
    sides = [((0, NEAR), (NEAR, width - NEAR)) for _, width in PARTS]
    g1, g2, sel, got, outs, back, p2, f2, p1, f1, sums = (rest[i * count : (i + 1) * count] for i in range(11))
    pick, mix_hi, mix_lo, tokens, inner, local_sem, send_sem, recv_sem = rest[11 * count :]

    me = lax.axis_index("ep")
    place = (me // 32, (me // 8) % 4, (me // 2) % 4)
    core = me % 2

    def device(dim, step, core_step=0):
        moved = (place[dim] + step) % SIDE
        other = (core + core_step) % 2
        return me + (moved - place[dim]) * STRIDES[dim] + (other - core)

    loads = [
        pltpu.make_async_copy(queries.at[0], q_buf, local_sem.at[0]),
        pltpu.make_async_copy(cache, c_buf, local_sem.at[1]),
        pltpu.make_async_copy(gate_w.at[0], wg, local_sem.at[2]),
        pltpu.make_async_copy(up_w.at[0], wu, local_sem.at[3]),
        pltpu.make_async_copy(turns, turn_buf, local_sem.at[4]),
        pltpu.make_async_copy(down_w.at[0], wd, local_sem.at[5]),
    ]
    for load in loads:
        load.start()

    barrier = pltpu.get_barrier_semaphore()
    partners = [device(dim, step, c) for dim in range(3) for step in range(1, SIDE) for c in range(2)]
    partners.append(device(0, 0, 1))
    for partner in partners:
        pl.semaphore_signal(barrier, inc=1, device_id=(partner,), device_id_type=MESH)

    hidden_f = hidden[0].astype(F32)
    mean_square = jnp.mean(hidden_f * hidden_f, axis=-1, keepdims=True)
    normed = (hidden_f * lax.rsqrt(mean_square + 1e-06) * gain[...].reshape(1, D)).astype(BF16)
    lanes = lax.broadcasted_iota(jnp.int32, (ROWS, META), 1)
    both = jnp.concatenate([routes[0].astype(F32), route_weight[0]], axis=0)
    both = jnp.transpose(both)
    route_now = both[:, 0:TOPK].astype(jnp.int32)
    weight_now = both[:, TOPK : 2 * TOPK]
    named = [lanes == route_now[:, k : k + 1] for k in range(TOPK)]
    taken = sum(hit.astype(F32) for hit in named)
    earlier = lax.broadcasted_iota(jnp.int32, (ROWS, ROWS), 0) > lax.broadcasted_iota(jnp.int32, (ROWS, ROWS), 1)
    before = dot(earlier.astype(BF16), taken.astype(BF16))
    meta = jnp.zeros((ROWS, META), F32)
    for k in range(TOPK):
        rank = jnp.sum(jnp.where(named[k], before, 0.0), axis=1, keepdims=True)
        weight = weight_now[:, k : k + 1]
        high = weight.astype(BF16).astype(F32)
        meta = jnp.where(lanes == k, route_now[:, k : k + 1].astype(F32), meta)
        meta = jnp.where(lanes == TOPK + k, rank, meta)
        meta = jnp.where(lanes == 2 * TOPK + k, high, meta)
        meta = jnp.where(lanes == 3 * TOPK + k, weight - high, meta)
    meta = meta.astype(BF16)
    for p, (first, width) in enumerate(PARTS):
        g1[p][0:ROWS, 0:NEAR] = normed[:, first : first + NEAR]
        g1[p][0:ROWS, NEAR : NEAR + META] = meta
        g1[p][0:ROWS, NEAR + META :] = normed[:, first + NEAR : first + width]

    pl.semaphore_wait(barrier, len(partners))

    def remote(src, dst, p, group, target):
        return pltpu.make_async_remote_copy(
            src_ref=src, dst_ref=dst, send_sem=send_sem.at[p, group], recv_sem=recv_sem.at[p, group],
            device_id=(target,), device_id_type=MESH,
        )

    def landing(p, group):
        width = PARTS[p][1]
        near, far = pl.ds(0, NEAR), pl.ds(NEAR, width - NEAR)
        return (
            g1[p].at[pl.ds(ROWS, 48)], g1[p].at[pl.ds(ROWS, 48)],
            g2[p].at[pl.ds(0, 144), pl.ds(0, NEAR + META)], g2[p].at[pl.ds(0, 144), pl.ds(NEAR + META, width - NEAR)],
            got[p].at[pl.ds(SLOTS, HALF - SLOTS)], got[p].at[pl.ds(HALF, HALF)],
            back[p].at[pl.ds(SLOTS, HALF - SLOTS)],
            back[p].at[pl.ds(HALF, HALF), near], back[p].at[pl.ds(HALF, HALF), far],
            f2[p].at[pl.ds(64, 192), near], f2[p].at[pl.ds(64, 192), far],
            f1[p].at[pl.ds(ROWS, 48)],
        )[group]

    def arrived(p, group):
        remote(landing(p, group), landing(p, group), p, group, device(0, 1)).wait_recv()

    def left(p, group):
        remote(landing(p, group), landing(p, group), p, group, device(0, 1)).wait_send()

    def block(ref, number, rows):
        return ref.at[pl.ds(number * rows, rows)]

    for p in range(count):
        for k in (2, 1, 3):
            remote(block(g1[p], 0, ROWS), block(g1[p], k, ROWS), p, 0, device(ORDERS[p][0], k)).start()
    for p in range(count):
        for k in (2, 1, 3):
            remote(
                block(g1[p], 0, ROWS), g2[p].at[pl.ds(64 * k, ROWS)], p, 1, device(ORDERS[p][1], k)
            ).start()

    loads[0].wait()
    loads[1].wait()

    def attend(row, unused):
        q = q_buf[row]
        keys = c_buf[row]
        new = fresh[0]
        scores = dot(q, keys) * soft_scale
        scores = jnp.where(lax.broadcasted_iota(jnp.int32, (HEADS, CTX), 1) < lengths[row], scores, neg_large)
        new_scores = dot_t(q, new) * soft_scale
        new_scores = jnp.where(lax.broadcasted_iota(jnp.int32, (HEADS, ROWS), 1) == row, new_scores, neg_large)
        most = jnp.maximum(jnp.max(scores, axis=1, keepdims=True), jnp.max(new_scores, axis=1, keepdims=True))
        weight = jnp.exp(scores - most)
        new_weight = jnp.exp(new_scores - most)
        total = jnp.sum(weight, axis=1, keepdims=True) + jnp.sum(new_weight, axis=1, keepdims=True)
        summed = dot_t(weight.astype(BF16), keys[:LAT]) + dot(new_weight.astype(BF16), new[:, :LAT])
        att_buf[row] = (summed / total).astype(BF16)
        return unused

    lax.fori_loop(0, 2, attend, 0)

    for side in range(2):
        for p, (_, width) in enumerate(PARTS):
            if side == 0:
                arrived(p, 0)
            columns = (pl.ds(0, NEAR + META), pl.ds(NEAR + META, width - NEAR))[side]
            for k in (2, 1, 3):
                remote(
                    g1[p].at[pl.ds(ROWS, 48), columns], g2[p].at[pl.ds(64 * k + ROWS, 48), columns],
                    p, 2 + side, device(ORDERS[p][1], k),
                ).start()
    for p in range(count):
        g2[p][0:64, :] = g1[p][...]

    lax.fori_loop(2, 8, attend, 0)

    def targets(p, shape, dim):
        index = lax.broadcasted_iota(jnp.int32, shape, dim)
        goal = jnp.zeros(shape, jnp.int32)
        for number in range(LINE):
            expert = device(ORDERS[p][2], number % SIDE, number // SIDE)
            inside = index - number * SLOTS
            rank = (inside >= 16).astype(jnp.int32) + (inside >= 32).astype(jnp.int32)
            code = (inside - rank * 16) * 512 + expert * 4 + rank
            goal = jnp.where((inside >= 0) & (inside < SLOTS), code, goal)
        return goal.astype(F32)

    def picked(p, half, side):
        first, width = sides[p][side]
        source = first + META * side
        rows = dot(pick[p, half * HALF : half * HALF + HALF, :], g2[p][:, source : source + width]).astype(BF16)
        if half == 0:
            got[p][0:SLOTS, first : first + width] = rows[0:SLOTS]
            sel[p][0 : HALF - SLOTS, first : first + width] = rows[SLOTS:]
        else:
            sel[p][HALF - SLOTS :, first : first + width] = rows

    def send_picked(p, half):
        for step in (2, 1, 3) if half == 0 else (2, 1, 3, 0):
            number = half * SIDE + step
            remote(
                block(sel[p], number - 1, SLOTS), block(got[p], number, SLOTS), p, 4 + half,
                device(ORDERS[p][2], step, half),
            ).start()

    for p in range(count):
        arrived(p, 1)
        arrived(p, 2)
        meta_t = jnp.transpose(g2[p][:, NEAR : NEAR + META].astype(F32))
        home = (lax.broadcasted_iota(jnp.int32, (TOPK, 256), 1) // 16) * 512
        codes = meta_t[0:TOPK] * 4.0 + meta_t[TOPK : 2 * TOPK] + home.astype(F32)
        goal = targets(p, (ALL, 1), 0)
        hit = jnp.zeros((ALL, 256), F32)
        for k in range(TOPK):
            hit = jnp.where(codes[k : k + 1] == goal, 1.0, hit)
        pick[p] = hit.astype(BF16)
        picked(p, 0, 0)
    for p in range(count):
        arrived(p, 3)
        picked(p, 0, 1)
        send_picked(p, 0)
    for p in range(count):
        picked(p, 1, 0)
        picked(p, 1, 1)
        send_picked(p, 1)

    for p in range(count):
        meta_all = g2[p][:, NEAR : NEAR + META].astype(F32)
        home = (lax.broadcasted_iota(jnp.int32, (256, 1), 0) // 16) * 512
        goal = targets(p, (1, ALL), 1)
        share = jnp.zeros((256, ALL), F32)
        for k in range(TOPK):
            code = meta_all[:, k : k + 1] * 4.0 + meta_all[:, TOPK + k : TOPK + k + 1] + home.astype(F32)
            weight = meta_all[:, 2 * TOPK + k : 2 * TOPK + k + 1] + meta_all[:, 3 * TOPK + k : 3 * TOPK + k + 1]
            share = jnp.where(code == goal, weight, share)
        high = share.astype(BF16)
        low = (share - high.astype(F32)).astype(BF16)
        for half in range(2):
            mix_hi[p, half] = high[:, half * HALF : half * HALF + HALF]
            mix_lo[p, half] = low[:, half * HALF : half * HALF + HALF]

    lax.fori_loop(8, 12, attend, 0)

    loads[4].wait()
    def send_back(p, half, columns, group):
        for step in (2, 1, 3) if half == 0 else (2, 1, 3, 0):
            number = half * SIDE + step
            remote(
                outs[p].at[pl.ds((number - 1) * SLOTS, SLOTS), columns],
                back[p].at[pl.ds(number * SLOTS, SLOTS), columns], p, group, device(ORDERS[p][2], -step, half),
            ).start()

    for half in range(2):
        for p, (first, width) in enumerate(PARTS):
            arrived(p, 4 + half)
            rows = got[p][half * HALF : half * HALF + HALF, :]
            if p:
                rows = dot(turn_buf[p - 1], rows).astype(BF16)
            tokens[:, first : first + width] = rows
        if half == 0:
            loads[2].wait()
            loads[3].wait()
        gate = dot(tokens[...], wg[...])
        up = dot(tokens[...], wu[...])
        inner[0] = (gate / (1.0 + jnp.exp(-gate)) * up).astype(BF16)
        if half == 0:
            loads[5].wait()
        for p in (1, 2):
            inner[p] = dot(turn_buf[2 - p], inner[0]).astype(BF16)
        if half == 0:
            for p, (first, width) in enumerate(PARTS):
                result = dot(inner[p], wd[:, first : first + width]).astype(BF16)
                back[p][0:SLOTS, :] = result[0:SLOTS]
                outs[p][0 : HALF - SLOTS, :] = result[SLOTS:]
                send_back(p, 0, pl.ds(0, width), 6)
        else:
            for side in range(2):
                for p, (first, _) in enumerate(PARTS):
                    begin, width = sides[p][side]
                    result = dot(inner[p], wd[:, first + begin : first + begin + width]).astype(BF16)
                    outs[p][HALF - SLOTS :, begin : begin + width] = result
                    send_back(p, 1, pl.ds(begin, width), 7 + side)

    def relay_sum(p, half, begin, width):
        rows = back[p][half * HALF : half * HALF + HALF, begin : begin + width]
        return dot(mix_hi[p, half], rows) + dot(mix_lo[p, half], rows)

    for p, (_, width) in enumerate(PARTS):
        arrived(p, 6)
        sums[p][...] = relay_sum(p, 0, 0, width)
    for side in range(2):
        for p in range(count):
            begin, width = sides[p][side]
            arrived(p, 7 + side)
            columns = slice(begin, begin + width)
            summed = (sums[p][:, columns] + relay_sum(p, 1, begin, width)).astype(BF16)
            f2[p][0:64, columns] = summed[0:64]
            p2[p][:, columns] = summed[64:]
            for k in (2, 1, 3):
                remote(
                    p2[p].at[pl.ds(64 * (k - 1), 64), pl.ds(begin, width)],
                    f2[p].at[pl.ds(64 * k, 64), pl.ds(begin, width)], p, 9 + side, device(ORDERS[p][1], -k),
                ).start()

    lax.fori_loop(12, ROWS, attend, 0)
    store = pltpu.make_async_copy(att_buf, attended.at[0], local_sem.at[6])
    store.start()

    for side in range(2):
        for p in range(count):
            begin, width = sides[p][side]
            arrived(p, 9 + side)
            columns = slice(begin, begin + width)
            summed = sum(f2[p][64 * k : 64 * k + 64, columns].astype(F32) for k in range(SIDE)).astype(BF16)
            f1[p][0:ROWS, columns] = summed[0:ROWS]
            p1[p][:, columns] = summed[ROWS:]
            if side:
                for k in (2, 1, 3):
                    remote(
                        block(p1[p], k - 1, ROWS), block(f1[p], k, ROWS), p, 11, device(ORDERS[p][0], -k)
                    ).start()

    for p, (first, width) in enumerate(PARTS):
        arrived(p, 11)
        summed = sum(f1[p][ROWS * k : ROWS * k + ROWS, :].astype(F32) for k in range(SIDE))
        mix[0, :, first : first + width] = summed.astype(BF16)

    for p in range(count):
        for group in range(12):
            left(p, group)
    store.wait()


def finish(attended, mix, attended_out, mix_out, att_buf, mix_buf, sem):
    pieces, rows = 4, ROWS // 4
    loads = [pltpu.make_async_copy(mix, mix_buf, sem.at[pieces])]
    stores = [pltpu.make_async_copy(mix_buf, mix_out, sem.at[2 * pieces + 1])]
    for i in range(pieces):
        part = pl.ds(i * rows, rows)
        loads.append(pltpu.make_async_copy(attended.at[0, part], att_buf.at[part], sem.at[i]))
        stores.append(pltpu.make_async_copy(att_buf.at[part], attended_out.at[0, part], sem.at[pieces + 1 + i]))
    for load in loads:
        load.start()
    for load, store in zip(loads, stores):
        load.wait()
        store.start()
    for store in stores:
        store.wait()


def on_device(
    queries, latent_cache, new_latent, lengths, hidden, norm_gain, routes, route_weight, gate_weight, up_weight,
    down_weight,
):
    def per_part(rows, extra=0, dtype=BF16):
        return [pltpu.VMEM((rows, width + extra), dtype) for _, width in PARTS]

    vmem = pl.BlockSpec(memory_space=pltpu.VMEM)
    smem = pl.BlockSpec(memory_space=pltpu.SMEM)
    hbm = pl.BlockSpec(memory_space=pl.ANY)
    turns = jnp.asarray(slot_orders(), BF16)
    results = pl.pallas_call(
        kernel,
        out_shape=(
            jax.ShapeDtypeStruct((1, ROWS, HEADS, LAT), BF16),
            jax.ShapeDtypeStruct((1, ROWS, D), BF16),
        ),
        in_specs=[smem, vmem, vmem, vmem, vmem, vmem] + [hbm] * 6,
        out_specs=(hbm, vmem),
        scratch_shapes=[
            pltpu.VMEM((ROWS, HEADS, KDIM), BF16),
            pltpu.VMEM((ROWS, KDIM, CTX), BF16),
            pltpu.VMEM((ROWS, HEADS, LAT), BF16),
            pltpu.VMEM((2, HALF, HALF), BF16),
            pltpu.VMEM((D, FF), BF16),
            pltpu.VMEM((D, FF), BF16),
            pltpu.VMEM((FF, D), BF16),
            *per_part(64, META),
            *per_part(256, META),
            *per_part(ALL - SLOTS),
            *per_part(ALL),
            *per_part(ALL - SLOTS),
            *per_part(ALL),
            *per_part(192),
            *per_part(256),
            *per_part(48),
            *per_part(64),
            *per_part(256, dtype=F32),
            pltpu.VMEM((3, ALL, 256), BF16),
            pltpu.VMEM((3, 2, 256, HALF), BF16),
            pltpu.VMEM((3, 2, 256, HALF), BF16),
            pltpu.VMEM((HALF, D), BF16),
            pltpu.VMEM((3, HALF, FF), BF16),
            pltpu.SemaphoreType.DMA((7,)),
            pltpu.SemaphoreType.DMA((3, 12)),
            pltpu.SemaphoreType.DMA((3, 12)),
        ],
        compiler_params=pltpu.CompilerParams(
            collective_id=0, has_side_effects=True, vmem_limit_bytes=61 * 2**20
        ),
    )(
        lengths, new_latent, hidden, norm_gain, jnp.swapaxes(routes, 1, 2), jnp.swapaxes(route_weight, 1, 2), queries,
        jnp.swapaxes(latent_cache, 1, 2), turns, gate_weight, up_weight, down_weight,
    )
    return pl.pallas_call(
        finish,
        out_shape=(
            jax.ShapeDtypeStruct((1, ROWS, HEADS, LAT), BF16),
            jax.ShapeDtypeStruct((1, ROWS, D), BF16),
        ),
        in_specs=[hbm, hbm],
        out_specs=(hbm, hbm),
        scratch_shapes=[
            pltpu.VMEM((ROWS, HEADS, LAT), BF16),
            pltpu.VMEM((1, ROWS, D), BF16),
            pltpu.SemaphoreType.DMA((10,)),
        ],
    )(*results)


def solution(mesh):
    placed = (
        P(None, "ep", None, None),
        P("ep", None, None),
        P(None, "ep", None),
        P("ep"),
        P(None, "ep", None),
        P(),
        P(None, "ep", None),
        P(None, "ep", None),
        P("ep", None, None),
        P("ep", None, None),
        P("ep", None, None),
    )
    return jax.shard_map(
        on_device,
        mesh=mesh,
        in_specs=placed,
        out_specs=(P(None, "ep", None, None), P(None, "ep", None)),
        check_vma=False,
    )
```

```python
import functools

import jax
import jax.numpy as jnp
import numpy as np
from jax import lax
from jax.experimental import pallas as pl
from jax.experimental.pallas import tpu as pltpu
from jax.sharding import PartitionSpec as P

MESH = pl.DeviceIdType.MESH
F32, BF16 = jnp.float32, jnp.bfloat16

D, FF, HEADS, LAT, KDIM, TOPK, CTX, ROWS = 3584, 1024, 64, 512, 576, 8, 128, 16
MOST = 3
SIDE = 4
SLOTS = MOST * SIDE * SIDE
LINE = 2 * SIDE
ALL = SLOTS * LINE
META = 128
soft_scale = 192.0 ** (-0.5)
neg_large = -1e30

ORDERS = ((0, 1, 2), (1, 2, 0), (2, 0, 1))
PARTS = ((0, 1280), (1280, 1152), (2432, 1152))
NEAR = 640
STRIDES = (32, 8, 2)
HALF = ALL // 2


def slot_orders():
    def row(k1, k2, k3, j):
        return k3 * SLOTS + j * SIDE * SIDE + k2 * SIDE + k1

    turns = np.zeros((2, HALF, HALF), np.float32)
    for ky in range(SIDE):
        for kz in range(SIDE):
            for kx in range(SIDE):
                for j in range(MOST):
                    k = (ky, kz, kx)
                    rows = [row(k[o[0]], k[o[1]], k[o[2]], j) for o in ORDERS]
                    turns[0, rows[0], rows[1]] = 1
                    turns[1, rows[0], rows[2]] = 1
    return turns


def dot(a, b):
    return jnp.dot(a, b, preferred_element_type=F32)


def dot_t(a, b):
    return lax.dot_general(a, b, (((1,), (1,)), ((), ())), preferred_element_type=F32)


def kernel(
    lengths, fresh, hidden, gain, routes, route_weight, queries, cache, turns, gate_w, up_w, down_w,
    attended, mix,
    q_buf, c_buf, att_buf, turn_buf, wg, wu, wd, *rest,
):
    count = len(PARTS)
    sides = [((0, NEAR), (NEAR, width - NEAR)) for _, width in PARTS]
    g1, g2, sel, got, outs, back, p2, f2, p1, f1, sums = (rest[i * count : (i + 1) * count] for i in range(11))
    pick, mix_hi, mix_lo, tokens, inner, local_sem, send_sem, recv_sem = rest[11 * count :]

    me = lax.axis_index("ep")
    place = (me // 32, (me // 8) % 4, (me // 2) % 4)
    core = me % 2

    def device(dim, step, core_step=0):
        moved = (place[dim] + step) % SIDE
        other = (core + core_step) % 2
        return me + (moved - place[dim]) * STRIDES[dim] + (other - core)

    loads = [
        pltpu.make_async_copy(queries.at[0], q_buf, local_sem.at[0]),
        pltpu.make_async_copy(cache, c_buf, local_sem.at[1]),
        pltpu.make_async_copy(gate_w.at[0], wg, local_sem.at[2]),
        pltpu.make_async_copy(up_w.at[0], wu, local_sem.at[3]),
        pltpu.make_async_copy(turns, turn_buf, local_sem.at[4]),
        pltpu.make_async_copy(down_w.at[0], wd, local_sem.at[5]),
    ]
    for load in loads:
        load.start()

    barrier = pltpu.get_barrier_semaphore()
    partners = [device(dim, step, c) for dim in range(3) for step in range(1, SIDE) for c in range(2)]
    partners.append(device(0, 0, 1))
    for partner in partners:
        pl.semaphore_signal(barrier, inc=1, device_id=(partner,), device_id_type=MESH)

    hidden_f = hidden[0].astype(F32)
    mean_square = jnp.mean(hidden_f * hidden_f, axis=-1, keepdims=True)
    normed = (hidden_f * lax.rsqrt(mean_square + 1e-06) * gain[...].reshape(1, D)).astype(BF16)
    lanes = lax.broadcasted_iota(jnp.int32, (ROWS, META), 1)
    both = jnp.concatenate([routes[0].astype(F32), route_weight[0]], axis=0)
    both = jnp.transpose(both)
    route_now = both[:, 0:TOPK].astype(jnp.int32)
    weight_now = both[:, TOPK : 2 * TOPK]
    named = [lanes == route_now[:, k : k + 1] for k in range(TOPK)]
    taken = sum(hit.astype(F32) for hit in named)
    earlier = lax.broadcasted_iota(jnp.int32, (ROWS, ROWS), 0) > lax.broadcasted_iota(jnp.int32, (ROWS, ROWS), 1)
    before = dot(earlier.astype(BF16), taken.astype(BF16))
    meta = jnp.zeros((ROWS, META), F32)
    for k in range(TOPK):
        rank = jnp.sum(jnp.where(named[k], before, 0.0), axis=1, keepdims=True)
        weight = weight_now[:, k : k + 1]
        high = weight.astype(BF16).astype(F32)
        meta = jnp.where(lanes == k, route_now[:, k : k + 1].astype(F32), meta)
        meta = jnp.where(lanes == TOPK + k, rank, meta)
        meta = jnp.where(lanes == 2 * TOPK + k, high, meta)
        meta = jnp.where(lanes == 3 * TOPK + k, weight - high, meta)
    meta = meta.astype(BF16)
    for p, (first, width) in enumerate(PARTS):
        g1[p][0:ROWS, 0:NEAR] = normed[:, first : first + NEAR]
        g1[p][0:ROWS, NEAR : NEAR + META] = meta
        g1[p][0:ROWS, NEAR + META :] = normed[:, first + NEAR : first + width]

    pl.semaphore_wait(barrier, len(partners))

    def remote(src, dst, p, group, target):
        return pltpu.make_async_remote_copy(
            src_ref=src, dst_ref=dst, send_sem=send_sem.at[p, group], recv_sem=recv_sem.at[p, group],
            device_id=(target,), device_id_type=MESH,
        )

    def landing(p, group):
        width = PARTS[p][1]
        near, far = pl.ds(0, NEAR), pl.ds(NEAR, width - NEAR)
        return (
            g1[p].at[pl.ds(ROWS, 48)], g1[p].at[pl.ds(ROWS, 48)],
            g2[p].at[pl.ds(0, 144), pl.ds(0, NEAR + META)], g2[p].at[pl.ds(0, 144), pl.ds(NEAR + META, width - NEAR)],
            got[p].at[pl.ds(SLOTS, HALF - SLOTS)], got[p].at[pl.ds(HALF, HALF)],
            back[p].at[pl.ds(SLOTS, HALF - SLOTS)],
            back[p].at[pl.ds(HALF, HALF), near], back[p].at[pl.ds(HALF, HALF), far],
            f2[p].at[pl.ds(64, 192), near], f2[p].at[pl.ds(64, 192), far],
            f1[p].at[pl.ds(ROWS, 48)],
        )[group]

    def arrived(p, group):
        remote(landing(p, group), landing(p, group), p, group, device(0, 1)).wait_recv()

    def left(p, group):
        remote(landing(p, group), landing(p, group), p, group, device(0, 1)).wait_send()

    def block(ref, number, rows):
        return ref.at[pl.ds(number * rows, rows)]

    for p in range(count):
        for k in (2, 1, 3):
            remote(block(g1[p], 0, ROWS), block(g1[p], k, ROWS), p, 0, device(ORDERS[p][0], k)).start()
    loads[0].wait()
    loads[1].wait()

    def attend(row, unused):
        q = q_buf[row]
        keys = c_buf[row]
        new = fresh[0]
        scores = dot(q, keys) * soft_scale
        scores = jnp.where(lax.broadcasted_iota(jnp.int32, (HEADS, CTX), 1) < lengths[row], scores, neg_large)
        new_scores = dot_t(q, new) * soft_scale
        new_scores = jnp.where(lax.broadcasted_iota(jnp.int32, (HEADS, ROWS), 1) == row, new_scores, neg_large)
        most = jnp.maximum(jnp.max(scores, axis=1, keepdims=True), jnp.max(new_scores, axis=1, keepdims=True))
        weight = jnp.exp(scores - most)
        new_weight = jnp.exp(new_scores - most)
        total = jnp.sum(weight, axis=1, keepdims=True) + jnp.sum(new_weight, axis=1, keepdims=True)
        summed = dot_t(weight.astype(BF16), keys[:LAT]) + dot(new_weight.astype(BF16), new[:, :LAT])
        att_buf[row] = (summed / total).astype(BF16)
        return unused

    lax.fori_loop(0, 2, attend, 0)

    for p in range(count):
        for k in (2, 1, 3):
            remote(
                block(g1[p], 0, ROWS), g2[p].at[pl.ds(64 * k, ROWS)], p, 1, device(ORDERS[p][1], k)
            ).start()

    for side in range(2):
        for p, (_, width) in enumerate(PARTS):
            if side == 0:
                arrived(p, 0)
            columns = (pl.ds(0, NEAR + META), pl.ds(NEAR + META, width - NEAR))[side]
            for k in (2, 1, 3):
                remote(
                    g1[p].at[pl.ds(ROWS, 48), columns], g2[p].at[pl.ds(64 * k + ROWS, 48), columns],
                    p, 2 + side, device(ORDERS[p][1], k),
                ).start()
    for p in range(count):
        g2[p][0:64, :] = g1[p][...]

    lax.fori_loop(2, 8, attend, 0)

    def targets(p, shape, dim):
        index = lax.broadcasted_iota(jnp.int32, shape, dim)
        goal = jnp.zeros(shape, jnp.int32)
        for number in range(LINE):
            expert = device(ORDERS[p][2], number % SIDE, number // SIDE)
            inside = index - number * SLOTS
            rank = (inside >= 16).astype(jnp.int32) + (inside >= 32).astype(jnp.int32)
            code = (inside - rank * 16) * 512 + expert * 4 + rank
            goal = jnp.where((inside >= 0) & (inside < SLOTS), code, goal)
        return goal.astype(F32)

    def picked(p, half, side):
        first, width = sides[p][side]
        source = first + META * side
        rows = dot(pick[p, half * HALF : half * HALF + HALF, :], g2[p][:, source : source + width]).astype(BF16)
        if half == 0:
            got[p][0:SLOTS, first : first + width] = rows[0:SLOTS]
            sel[p][0 : HALF - SLOTS, first : first + width] = rows[SLOTS:]
        else:
            sel[p][HALF - SLOTS :, first : first + width] = rows

    def send_picked(p, half):
        for step in (2, 1, 3) if half == 0 else (2, 1, 3, 0):
            number = half * SIDE + step
            remote(
                block(sel[p], number - 1, SLOTS), block(got[p], number, SLOTS), p, 4 + half,
                device(ORDERS[p][2], step, half),
            ).start()

    for p in range(count):
        arrived(p, 1)
        arrived(p, 2)
        meta_t = jnp.transpose(g2[p][:, NEAR : NEAR + META].astype(F32))
        home = (lax.broadcasted_iota(jnp.int32, (TOPK, 256), 1) // 16) * 512
        codes = meta_t[0:TOPK] * 4.0 + meta_t[TOPK : 2 * TOPK] + home.astype(F32)
        goal = targets(p, (ALL, 1), 0)
        hit = jnp.zeros((ALL, 256), F32)
        for k in range(TOPK):
            hit = jnp.where(codes[k : k + 1] == goal, 1.0, hit)
        pick[p] = hit.astype(BF16)
        picked(p, 0, 0)
    for p in range(count):
        arrived(p, 3)
        picked(p, 0, 1)
        send_picked(p, 0)
    for p in range(count):
        meta_all = g2[p][:, NEAR : NEAR + META].astype(F32)
        home = (lax.broadcasted_iota(jnp.int32, (256, 1), 0) // 16) * 512
        goal = targets(p, (1, ALL), 1)
        share = jnp.zeros((256, ALL), F32)
        for k in range(TOPK):
            code = meta_all[:, k : k + 1] * 4.0 + meta_all[:, TOPK + k : TOPK + k + 1] + home.astype(F32)
            weight = meta_all[:, 2 * TOPK + k : 2 * TOPK + k + 1] + meta_all[:, 3 * TOPK + k : 3 * TOPK + k + 1]
            share = jnp.where(code == goal, weight, share)
        high = share.astype(BF16)
        low = (share - high.astype(F32)).astype(BF16)
        for half in range(2):
            mix_hi[p, half] = high[:, half * HALF : half * HALF + HALF]
            mix_lo[p, half] = low[:, half * HALF : half * HALF + HALF]

    lax.fori_loop(8, 12, attend, 0)

    for p in range(count):
        picked(p, 1, 0)
        picked(p, 1, 1)
        send_picked(p, 1)


    loads[4].wait()
    def send_back(p, half, columns, group):
        for step in (2, 1, 3) if half == 0 else (2, 1, 3, 0):
            number = half * SIDE + step
            remote(
                outs[p].at[pl.ds((number - 1) * SLOTS, SLOTS), columns],
                back[p].at[pl.ds(number * SLOTS, SLOTS), columns], p, group, device(ORDERS[p][2], -step, half),
            ).start()

    for half in range(2):
        for p, (first, width) in enumerate(PARTS):
            arrived(p, 4 + half)
            rows = got[p][half * HALF : half * HALF + HALF, :]
            if p:
                rows = dot(turn_buf[p - 1], rows).astype(BF16)
            tokens[:, first : first + width] = rows
        if half == 0:
            loads[2].wait()
            loads[3].wait()
        gate = dot(tokens[...], wg[...])
        up = dot(tokens[...], wu[...])
        inner[0] = (gate / (1.0 + jnp.exp(-gate)) * up).astype(BF16)
        if half == 0:
            loads[5].wait()
        for p in (1, 2):
            inner[p] = dot(turn_buf[2 - p], inner[0]).astype(BF16)
        if half == 0:
            for p, (first, width) in enumerate(PARTS):
                result = dot(inner[p], wd[:, first : first + width]).astype(BF16)
                back[p][0:SLOTS, :] = result[0:SLOTS]
                outs[p][0 : HALF - SLOTS, :] = result[SLOTS:]
                send_back(p, 0, pl.ds(0, width), 6)
        else:
            for side in range(2):
                for p, (first, _) in enumerate(PARTS):
                    begin, width = sides[p][side]
                    result = dot(inner[p], wd[:, first + begin : first + begin + width]).astype(BF16)
                    outs[p][HALF - SLOTS :, begin : begin + width] = result
                    send_back(p, 1, pl.ds(begin, width), 7 + side)

    def relay_sum(p, half, begin, width):
        rows = back[p][half * HALF : half * HALF + HALF, begin : begin + width]
        return dot(mix_hi[p, half], rows) + dot(mix_lo[p, half], rows)

    for p, (_, width) in enumerate(PARTS):
        arrived(p, 6)
        sums[p][...] = relay_sum(p, 0, 0, width)
    for side in range(2):
        for p in range(count):
            begin, width = sides[p][side]
            arrived(p, 7 + side)
            columns = slice(begin, begin + width)
            summed = (sums[p][:, columns] + relay_sum(p, 1, begin, width)).astype(BF16)
            f2[p][0:64, columns] = summed[0:64]
            p2[p][:, columns] = summed[64:]
            for k in (2, 1, 3):
                remote(
                    p2[p].at[pl.ds(64 * (k - 1), 64), pl.ds(begin, width)],
                    f2[p].at[pl.ds(64 * k, 64), pl.ds(begin, width)], p, 9 + side, device(ORDERS[p][1], -k),
                ).start()

    lax.fori_loop(12, ROWS, attend, 0)
    store = pltpu.make_async_copy(att_buf, attended.at[0], local_sem.at[6])
    store.start()

    for side in range(2):
        for p in range(count):
            begin, width = sides[p][side]
            arrived(p, 9 + side)
            columns = slice(begin, begin + width)
            summed = sum(f2[p][64 * k : 64 * k + 64, columns].astype(F32) for k in range(SIDE)).astype(BF16)
            f1[p][0:ROWS, columns] = summed[0:ROWS]
            p1[p][:, columns] = summed[ROWS:]
            if side:
                for k in (2, 1, 3):
                    remote(
                        block(p1[p], k - 1, ROWS), block(f1[p], k, ROWS), p, 11, device(ORDERS[p][0], -k)
                    ).start()

    for p, (first, width) in enumerate(PARTS):
        arrived(p, 11)
        summed = sum(f1[p][ROWS * k : ROWS * k + ROWS, :].astype(F32) for k in range(SIDE))
        mix[0, :, first : first + width] = summed.astype(BF16)

    for p in range(count):
        for group in range(12):
            left(p, group)
    store.wait()


def finish(attended, mix, attended_out, mix_out, att_buf, mix_buf, sem):
    pieces, rows = 4, ROWS // 4
    loads = [pltpu.make_async_copy(mix, mix_buf, sem.at[pieces])]
    stores = [pltpu.make_async_copy(mix_buf, mix_out, sem.at[2 * pieces + 1])]
    for i in range(pieces):
        part = pl.ds(i * rows, rows)
        loads.append(pltpu.make_async_copy(attended.at[0, part], att_buf.at[part], sem.at[i]))
        stores.append(pltpu.make_async_copy(att_buf.at[part], attended_out.at[0, part], sem.at[pieces + 1 + i]))
    for load in loads:
        load.start()
    for load, store in zip(loads, stores):
        load.wait()
        store.start()
    for store in stores:
        store.wait()


def on_device(
    queries, latent_cache, new_latent, lengths, hidden, norm_gain, routes, route_weight, gate_weight, up_weight,
    down_weight,
):
    def per_part(rows, extra=0, dtype=BF16):
        return [pltpu.VMEM((rows, width + extra), dtype) for _, width in PARTS]

    vmem = pl.BlockSpec(memory_space=pltpu.VMEM)
    smem = pl.BlockSpec(memory_space=pltpu.SMEM)
    hbm = pl.BlockSpec(memory_space=pl.ANY)
    turns = jnp.asarray(slot_orders(), BF16)
    results = pl.pallas_call(
        kernel,
        out_shape=(
            jax.ShapeDtypeStruct((1, ROWS, HEADS, LAT), BF16),
            jax.ShapeDtypeStruct((1, ROWS, D), BF16),
        ),
        in_specs=[smem, vmem, vmem, vmem, vmem, vmem] + [hbm] * 6,
        out_specs=(hbm, vmem),
        scratch_shapes=[
            pltpu.VMEM((ROWS, HEADS, KDIM), BF16),
            pltpu.VMEM((ROWS, KDIM, CTX), BF16),
            pltpu.VMEM((ROWS, HEADS, LAT), BF16),
            pltpu.VMEM((2, HALF, HALF), BF16),
            pltpu.VMEM((D, FF), BF16),
            pltpu.VMEM((D, FF), BF16),
            pltpu.VMEM((FF, D), BF16),
            *per_part(64, META),
            *per_part(256, META),
            *per_part(ALL - SLOTS),
            *per_part(ALL),
            *per_part(ALL - SLOTS),
            *per_part(ALL),
            *per_part(192),
            *per_part(256),
            *per_part(48),
            *per_part(64),
            *per_part(256, dtype=F32),
            pltpu.VMEM((3, ALL, 256), BF16),
            pltpu.VMEM((3, 2, 256, HALF), BF16),
            pltpu.VMEM((3, 2, 256, HALF), BF16),
            pltpu.VMEM((HALF, D), BF16),
            pltpu.VMEM((3, HALF, FF), BF16),
            pltpu.SemaphoreType.DMA((7,)),
            pltpu.SemaphoreType.DMA((3, 12)),
            pltpu.SemaphoreType.DMA((3, 12)),
        ],
        compiler_params=pltpu.CompilerParams(
            collective_id=0, has_side_effects=True, vmem_limit_bytes=61 * 2**20
        ),
    )(
        lengths, new_latent, hidden, norm_gain, jnp.swapaxes(routes, 1, 2), jnp.swapaxes(route_weight, 1, 2), queries,
        jnp.swapaxes(latent_cache, 1, 2), turns, gate_weight, up_weight, down_weight,
    )
    return pl.pallas_call(
        finish,
        out_shape=(
            jax.ShapeDtypeStruct((1, ROWS, HEADS, LAT), BF16),
            jax.ShapeDtypeStruct((1, ROWS, D), BF16),
        ),
        in_specs=[hbm, hbm],
        out_specs=(hbm, hbm),
        scratch_shapes=[
            pltpu.VMEM((ROWS, HEADS, LAT), BF16),
            pltpu.VMEM((1, ROWS, D), BF16),
            pltpu.SemaphoreType.DMA((10,)),
        ],
    )(*results)


def solution(mesh):
    placed = (
        P(None, "ep", None, None),
        P("ep", None, None),
        P(None, "ep", None),
        P("ep"),
        P(None, "ep", None),
        P(),
        P(None, "ep", None),
        P(None, "ep", None),
        P("ep", None, None),
        P("ep", None, None),
        P("ep", None, None),
    )
    return jax.shard_map(
        on_device,
        mesh=mesh,
        in_specs=placed,
        out_specs=(P(None, "ep", None, None), P(None, "ep", None)),
        check_vma=False,
    )
```

```python
import functools

import jax
import jax.numpy as jnp
import numpy as np
from jax import lax
from jax.experimental import pallas as pl
from jax.experimental.pallas import tpu as pltpu
from jax.sharding import PartitionSpec as P

MESH = pl.DeviceIdType.MESH
F32, BF16 = jnp.float32, jnp.bfloat16

D, FF, HEADS, LAT, KDIM, TOPK, CTX, ROWS = 3584, 1024, 64, 512, 576, 8, 128, 16
MOST = 3
SIDE = 4
SLOTS = MOST * SIDE * SIDE
LINE = 2 * SIDE
ALL = SLOTS * LINE
META = 128
soft_scale = 192.0 ** (-0.5)
neg_large = -1e30

ORDERS = ((0, 1, 2), (1, 2, 0), (2, 0, 1))
PARTS = ((0, 1280), (1280, 1152), (2432, 1152))
NEAR = 640
STRIDES = (32, 8, 2)
HALF = ALL // 2


def slot_orders():
    def row(k1, k2, k3, j):
        return k3 * SLOTS + j * SIDE * SIDE + k2 * SIDE + k1

    turns = np.zeros((2, HALF, HALF), np.float32)
    for ky in range(SIDE):
        for kz in range(SIDE):
            for kx in range(SIDE):
                for j in range(MOST):
                    k = (ky, kz, kx)
                    rows = [row(k[o[0]], k[o[1]], k[o[2]], j) for o in ORDERS]
                    turns[0, rows[0], rows[1]] = 1
                    turns[1, rows[0], rows[2]] = 1
    return turns


def dot(a, b):
    return jnp.dot(a, b, preferred_element_type=F32)


def dot_t(a, b):
    return lax.dot_general(a, b, (((1,), (1,)), ((), ())), preferred_element_type=F32)


def kernel(
    lengths, fresh, hidden, gain, routes, route_weight, queries, cache, turns, gate_w, up_w, down_w,
    attended, mix,
    q_buf, c_buf, att_buf, turn_buf, wg, wu, wd, *rest,
):
    count = len(PARTS)
    sides = [((0, NEAR), (NEAR, width - NEAR)) for _, width in PARTS]
    g1, g2, sel, got, outs, back, p2, f2, p1, f1, sums = (rest[i * count : (i + 1) * count] for i in range(11))
    pick, mix_hi, mix_lo, tokens, inner, local_sem, send_sem, recv_sem = rest[11 * count :]

    me = lax.axis_index("ep")
    place = (me // 32, (me // 8) % 4, (me // 2) % 4)
    core = me % 2

    def device(dim, step, core_step=0):
        moved = (place[dim] + step) % SIDE
        other = (core + core_step) % 2
        return me + (moved - place[dim]) * STRIDES[dim] + (other - core)

    loads = [
        pltpu.make_async_copy(queries.at[0], q_buf, local_sem.at[0]),
        pltpu.make_async_copy(cache, c_buf, local_sem.at[1]),
        pltpu.make_async_copy(gate_w.at[0], wg, local_sem.at[2]),
        pltpu.make_async_copy(up_w.at[0], wu, local_sem.at[3]),
        pltpu.make_async_copy(turns, turn_buf, local_sem.at[4]),
        pltpu.make_async_copy(down_w.at[0], wd, local_sem.at[5]),
    ]
    for load in loads:
        load.start()

    barrier = pltpu.get_barrier_semaphore()
    partners = [device(dim, step, c) for dim in range(3) for step in range(1, SIDE) for c in range(2)]
    partners.append(device(0, 0, 1))
    for partner in partners:
        pl.semaphore_signal(barrier, inc=1, device_id=(partner,), device_id_type=MESH)

    hidden_f = hidden[0].astype(F32)
    mean_square = jnp.mean(hidden_f * hidden_f, axis=-1, keepdims=True)
    normed = (hidden_f * lax.rsqrt(mean_square + 1e-06) * gain[...].reshape(1, D)).astype(BF16)
    lanes = lax.broadcasted_iota(jnp.int32, (ROWS, META), 1)
    both = jnp.concatenate([routes[0].astype(F32), route_weight[0]], axis=0)
    both = jnp.transpose(both)
    route_now = both[:, 0:TOPK].astype(jnp.int32)
    weight_now = both[:, TOPK : 2 * TOPK]
    named = [lanes == route_now[:, k : k + 1] for k in range(TOPK)]
    taken = sum(hit.astype(F32) for hit in named)
    earlier = lax.broadcasted_iota(jnp.int32, (ROWS, ROWS), 0) > lax.broadcasted_iota(jnp.int32, (ROWS, ROWS), 1)
    before = dot(earlier.astype(BF16), taken.astype(BF16))
    meta = jnp.zeros((ROWS, META), F32)
    for k in range(TOPK):
        rank = jnp.sum(jnp.where(named[k], before, 0.0), axis=1, keepdims=True)
        weight = weight_now[:, k : k + 1]
        high = weight.astype(BF16).astype(F32)
        meta = jnp.where(lanes == k, route_now[:, k : k + 1].astype(F32), meta)
        meta = jnp.where(lanes == TOPK + k, rank, meta)
        meta = jnp.where(lanes == 2 * TOPK + k, high, meta)
        meta = jnp.where(lanes == 3 * TOPK + k, weight - high, meta)
    meta = meta.astype(BF16)
    for p, (first, width) in enumerate(PARTS):
        g1[p][0:ROWS, 0:NEAR] = normed[:, first : first + NEAR]
        g1[p][0:ROWS, NEAR : NEAR + META] = meta
        g1[p][0:ROWS, NEAR + META :] = normed[:, first + NEAR : first + width]

    pl.semaphore_wait(barrier, len(partners))

    def departure(p, group):
        if group < 4:
            return 3 * min(group, 2) + p
        return 9 + (0, 1, 2, 3, 3, 4, 4, 5)[group - 4]

    def remote(src, dst, p, group, target):
        return pltpu.make_async_remote_copy(
            src_ref=src, dst_ref=dst, send_sem=send_sem.at[departure(p, group)], recv_sem=recv_sem.at[p, group],
            device_id=(target,), device_id_type=MESH,
        )

    def landing(p, group):
        width = PARTS[p][1]
        near, far = pl.ds(0, NEAR), pl.ds(NEAR, width - NEAR)
        return (
            g1[p].at[pl.ds(ROWS, 48)], g1[p].at[pl.ds(ROWS, 48)],
            g2[p].at[pl.ds(0, 144), pl.ds(0, NEAR + META)], g2[p].at[pl.ds(0, 144), pl.ds(NEAR + META, width - NEAR)],
            got[p].at[pl.ds(SLOTS, HALF - SLOTS)], got[p].at[pl.ds(HALF, HALF)],
            back[p].at[pl.ds(SLOTS, HALF - SLOTS)],
            back[p].at[pl.ds(HALF, HALF), near], back[p].at[pl.ds(HALF, HALF), far],
            f2[p].at[pl.ds(64, 192), near], f2[p].at[pl.ds(64, 192), far],
            f1[p].at[pl.ds(ROWS, 48)],
        )[group]

    def arrived(p, group):
        remote(landing(p, group), landing(p, group), p, group, device(0, 1)).wait_recv()

    def left(sent, p, group):
        remote(sent, sent, p, group, device(0, 1)).wait_send()

    def block(ref, number, rows):
        return ref.at[pl.ds(number * rows, rows)]

    for p in range(count):
        for k in (2, 1, 3):
            remote(block(g1[p], 0, ROWS), block(g1[p], k, ROWS), p, 0, device(ORDERS[p][0], k)).start()
    loads[0].wait()
    loads[1].wait()

    def attend(row, unused):
        q = q_buf[row]
        keys = c_buf[row]
        new = fresh[0]
        scores = dot(q, keys) * soft_scale
        scores = jnp.where(lax.broadcasted_iota(jnp.int32, (HEADS, CTX), 1) < lengths[row], scores, neg_large)
        new_scores = dot_t(q, new) * soft_scale
        new_scores = jnp.where(lax.broadcasted_iota(jnp.int32, (HEADS, ROWS), 1) == row, new_scores, neg_large)
        most = jnp.maximum(jnp.max(scores, axis=1, keepdims=True), jnp.max(new_scores, axis=1, keepdims=True))
        weight = jnp.exp(scores - most)
        new_weight = jnp.exp(new_scores - most)
        total = jnp.sum(weight, axis=1, keepdims=True) + jnp.sum(new_weight, axis=1, keepdims=True)
        summed = dot_t(weight.astype(BF16), keys[:LAT]) + dot(new_weight.astype(BF16), new[:, :LAT])
        att_buf[row] = (summed / total).astype(BF16)
        return unused

    lax.fori_loop(0, 2, attend, 0)

    for p in range(count):
        for k in (2, 1, 3):
            remote(
                block(g1[p], 0, ROWS), g2[p].at[pl.ds(64 * k, ROWS)], p, 1, device(ORDERS[p][1], k)
            ).start()

    for side in range(2):
        for p, (_, width) in enumerate(PARTS):
            if side == 0:
                arrived(p, 0)
            columns = (pl.ds(0, NEAR + META), pl.ds(NEAR + META, width - NEAR))[side]
            for k in (2, 1, 3):
                remote(
                    g1[p].at[pl.ds(ROWS, 48), columns], g2[p].at[pl.ds(64 * k + ROWS, 48), columns],
                    p, 2 + side, device(ORDERS[p][1], k),
                ).start()
    for p in range(count):
        g2[p][0:64, :] = g1[p][...]

    lax.fori_loop(2, 8, attend, 0)

    def targets(p, shape, dim):
        index = lax.broadcasted_iota(jnp.int32, shape, dim)
        goal = jnp.zeros(shape, jnp.int32)
        for number in range(LINE):
            expert = device(ORDERS[p][2], number % SIDE, number // SIDE)
            inside = index - number * SLOTS
            rank = (inside >= 16).astype(jnp.int32) + (inside >= 32).astype(jnp.int32)
            code = (inside - rank * 16) * 512 + expert * 4 + rank
            goal = jnp.where((inside >= 0) & (inside < SLOTS), code, goal)
        return goal.astype(F32)

    def picked(p, half, side):
        first, width = sides[p][side]
        source = first + META * side
        rows = dot(pick[p, half * HALF : half * HALF + HALF, :], g2[p][:, source : source + width]).astype(BF16)
        if half == 0:
            got[p][0:SLOTS, first : first + width] = rows[0:SLOTS]
            sel[p][0 : HALF - SLOTS, first : first + width] = rows[SLOTS:]
        else:
            sel[p][HALF - SLOTS :, first : first + width] = rows

    def send_picked(p, half):
        for step in (2, 1, 3) if half == 0 else (2, 1, 3, 0):
            number = half * SIDE + step
            remote(
                block(sel[p], number - 1, SLOTS), block(got[p], number, SLOTS), p, 4 + half,
                device(ORDERS[p][2], step, half),
            ).start()

    for p in range(count):
        arrived(p, 1)
        arrived(p, 2)
        meta_t = jnp.transpose(g2[p][:, NEAR : NEAR + META].astype(F32))
        home = (lax.broadcasted_iota(jnp.int32, (TOPK, 256), 1) // 16) * 512
        codes = meta_t[0:TOPK] * 4.0 + meta_t[TOPK : 2 * TOPK] + home.astype(F32)
        goal = targets(p, (ALL, 1), 0)
        hit = jnp.zeros((ALL, 256), F32)
        for k in range(TOPK):
            hit = jnp.where(codes[k : k + 1] == goal, 1.0, hit)
        pick[p] = hit.astype(BF16)
        picked(p, 0, 0)
    for p in range(count):
        arrived(p, 3)
        picked(p, 0, 1)
        send_picked(p, 0)
    for p in range(count):
        meta_all = g2[p][:, NEAR : NEAR + META].astype(F32)
        home = (lax.broadcasted_iota(jnp.int32, (256, 1), 0) // 16) * 512
        goal = targets(p, (1, ALL), 1)
        share = jnp.zeros((256, ALL), F32)
        for k in range(TOPK):
            code = meta_all[:, k : k + 1] * 4.0 + meta_all[:, TOPK + k : TOPK + k + 1] + home.astype(F32)
            weight = meta_all[:, 2 * TOPK + k : 2 * TOPK + k + 1] + meta_all[:, 3 * TOPK + k : 3 * TOPK + k + 1]
            share = jnp.where(code == goal, weight, share)
        high = share.astype(BF16)
        low = (share - high.astype(F32)).astype(BF16)
        for half in range(2):
            mix_hi[p, half] = high[:, half * HALF : half * HALF + HALF]
            mix_lo[p, half] = low[:, half * HALF : half * HALF + HALF]

    lax.fori_loop(8, 12, attend, 0)

    for p in range(count):
        picked(p, 1, 0)
        picked(p, 1, 1)
        send_picked(p, 1)


    loads[4].wait()
    def send_back(p, half, columns, group):
        for step in (2, 1, 3) if half == 0 else (2, 1, 3, 0):
            number = half * SIDE + step
            remote(
                outs[p].at[pl.ds((number - 1) * SLOTS, SLOTS), columns],
                back[p].at[pl.ds(number * SLOTS, SLOTS), columns], p, group, device(ORDERS[p][2], -step, half),
            ).start()

    for half in range(2):
        for p, (first, width) in enumerate(PARTS):
            arrived(p, 4 + half)
            rows = got[p][half * HALF : half * HALF + HALF, :]
            if p:
                rows = dot(turn_buf[p - 1], rows).astype(BF16)
            tokens[:, first : first + width] = rows
        if half == 0:
            loads[2].wait()
            loads[3].wait()
        gate = dot(tokens[...], wg[...])
        up = dot(tokens[...], wu[...])
        inner[0] = (gate / (1.0 + jnp.exp(-gate)) * up).astype(BF16)
        if half == 0:
            loads[5].wait()
        for p in (1, 2):
            inner[p] = dot(turn_buf[2 - p], inner[0]).astype(BF16)
        if half == 0:
            for p, (first, width) in enumerate(PARTS):
                result = dot(inner[p], wd[:, first : first + width]).astype(BF16)
                back[p][0:SLOTS, :] = result[0:SLOTS]
                outs[p][0 : HALF - SLOTS, :] = result[SLOTS:]
                send_back(p, 0, pl.ds(0, width), 6)
        else:
            for side in range(2):
                for p, (first, _) in enumerate(PARTS):
                    begin, width = sides[p][side]
                    result = dot(inner[p], wd[:, first + begin : first + begin + width]).astype(BF16)
                    outs[p][HALF - SLOTS :, begin : begin + width] = result
                    send_back(p, 1, pl.ds(begin, width), 7 + side)

    def relay_sum(p, half, begin, width):
        rows = back[p][half * HALF : half * HALF + HALF, begin : begin + width]
        return dot(mix_hi[p, half], rows) + dot(mix_lo[p, half], rows)

    for p, (_, width) in enumerate(PARTS):
        arrived(p, 6)
        sums[p][...] = relay_sum(p, 0, 0, width)
    for side in range(2):
        for p in range(count):
            begin, width = sides[p][side]
            arrived(p, 7 + side)
            columns = slice(begin, begin + width)
            summed = (sums[p][:, columns] + relay_sum(p, 1, begin, width)).astype(BF16)
            f2[p][0:64, columns] = summed[0:64]
            p2[p][:, columns] = summed[64:]
            for k in (2, 1, 3):
                remote(
                    p2[p].at[pl.ds(64 * (k - 1), 64), pl.ds(begin, width)],
                    f2[p].at[pl.ds(64 * k, 64), pl.ds(begin, width)], p, 9 + side, device(ORDERS[p][1], -k),
                ).start()

    lax.fori_loop(12, ROWS, attend, 0)
    store = pltpu.make_async_copy(att_buf, attended.at[0], local_sem.at[6])
    store.start()

    for side in range(2):
        for p in range(count):
            begin, width = sides[p][side]
            arrived(p, 9 + side)
            columns = slice(begin, begin + width)
            summed = sum(f2[p][64 * k : 64 * k + 64, columns].astype(F32) for k in range(SIDE)).astype(BF16)
            f1[p][0:ROWS, columns] = summed[0:ROWS]
            p1[p][:, columns] = summed[ROWS:]
            if side:
                for k in (2, 1, 3):
                    remote(
                        block(p1[p], k - 1, ROWS), block(f1[p], k, ROWS), p, 11, device(ORDERS[p][0], -k)
                    ).start()

    for p, (first, width) in enumerate(PARTS):
        arrived(p, 11)
        summed = sum(f1[p][ROWS * k : ROWS * k + ROWS, :].astype(F32) for k in range(SIDE))
        mix[0, :, first : first + width] = summed.astype(BF16)

    for p in range(count):
        left(landing(p, 0), p, 0)
        left(landing(p, 1), p, 1)
        left(g2[p].at[pl.ds(0, 144)], p, 2)
    for group, rows in ((4, HALF - SLOTS), (5, HALF), (6, HALF - SLOTS), (7, HALF), (9, HALF), (11, 48)):
        left(tokens.at[pl.ds(0, rows)], 0, group)
    store.wait()


def finish(attended, mix, attended_out, mix_out, att_buf, mix_buf, sem):
    pieces, rows = 4, ROWS // 4
    loads = [pltpu.make_async_copy(mix, mix_buf, sem.at[pieces])]
    stores = [pltpu.make_async_copy(mix_buf, mix_out, sem.at[2 * pieces + 1])]
    for i in range(pieces):
        part = pl.ds(i * rows, rows)
        loads.append(pltpu.make_async_copy(attended.at[0, part], att_buf.at[part], sem.at[i]))
        stores.append(pltpu.make_async_copy(att_buf.at[part], attended_out.at[0, part], sem.at[pieces + 1 + i]))
    for load in loads:
        load.start()
    for load, store in zip(loads, stores):
        load.wait()
        store.start()
    for store in stores:
        store.wait()


def on_device(
    queries, latent_cache, new_latent, lengths, hidden, norm_gain, routes, route_weight, gate_weight, up_weight,
    down_weight,
):
    def per_part(rows, extra=0, dtype=BF16):
        return [pltpu.VMEM((rows, width + extra), dtype) for _, width in PARTS]

    vmem = pl.BlockSpec(memory_space=pltpu.VMEM)
    smem = pl.BlockSpec(memory_space=pltpu.SMEM)
    hbm = pl.BlockSpec(memory_space=pl.ANY)
    turns = jnp.asarray(slot_orders(), BF16)
    results = pl.pallas_call(
        kernel,
        out_shape=(
            jax.ShapeDtypeStruct((1, ROWS, HEADS, LAT), BF16),
            jax.ShapeDtypeStruct((1, ROWS, D), BF16),
        ),
        in_specs=[smem, vmem, vmem, vmem, vmem, vmem] + [hbm] * 6,
        out_specs=(hbm, vmem),
        scratch_shapes=[
            pltpu.VMEM((ROWS, HEADS, KDIM), BF16),
            pltpu.VMEM((ROWS, KDIM, CTX), BF16),
            pltpu.VMEM((ROWS, HEADS, LAT), BF16),
            pltpu.VMEM((2, HALF, HALF), BF16),
            pltpu.VMEM((D, FF), BF16),
            pltpu.VMEM((D, FF), BF16),
            pltpu.VMEM((FF, D), BF16),
            *per_part(64, META),
            *per_part(256, META),
            *per_part(ALL - SLOTS),
            *per_part(ALL),
            *per_part(ALL - SLOTS),
            *per_part(ALL),
            *per_part(192),
            *per_part(256),
            *per_part(48),
            *per_part(64),
            *per_part(256, dtype=F32),
            pltpu.VMEM((3, ALL, 256), BF16),
            pltpu.VMEM((3, 2, 256, HALF), BF16),
            pltpu.VMEM((3, 2, 256, HALF), BF16),
            pltpu.VMEM((HALF, D), BF16),
            pltpu.VMEM((3, HALF, FF), BF16),
            pltpu.SemaphoreType.DMA((7,)),
            pltpu.SemaphoreType.DMA((15,)),
            pltpu.SemaphoreType.DMA((3, 12)),
        ],
        compiler_params=pltpu.CompilerParams(
            collective_id=0, has_side_effects=True, vmem_limit_bytes=61 * 2**20
        ),
    )(
        lengths, new_latent, hidden, norm_gain, jnp.swapaxes(routes, 1, 2), jnp.swapaxes(route_weight, 1, 2), queries,
        jnp.swapaxes(latent_cache, 1, 2), turns, gate_weight, up_weight, down_weight,
    )
    return pl.pallas_call(
        finish,
        out_shape=(
            jax.ShapeDtypeStruct((1, ROWS, HEADS, LAT), BF16),
            jax.ShapeDtypeStruct((1, ROWS, D), BF16),
        ),
        in_specs=[hbm, hbm],
        out_specs=(hbm, hbm),
        scratch_shapes=[
            pltpu.VMEM((ROWS, HEADS, LAT), BF16),
            pltpu.VMEM((1, ROWS, D), BF16),
            pltpu.SemaphoreType.DMA((10,)),
        ],
    )(*results)


def solution(mesh):
    placed = (
        P(None, "ep", None, None),
        P("ep", None, None),
        P(None, "ep", None),
        P("ep"),
        P(None, "ep", None),
        P(),
        P(None, "ep", None),
        P(None, "ep", None),
        P("ep", None, None),
        P("ep", None, None),
        P("ep", None, None),
    )
    return jax.shard_map(
        on_device,
        mesh=mesh,
        in_specs=placed,
        out_specs=(P(None, "ep", None, None), P(None, "ep", None)),
        check_vma=False,
    )
```
